32 devices in a mesh: dp: 4 (over x, core), clique: 8 (over z, y).
Axes of the slice: x: 2, y: 2, z: 4, core: 2. Of those that a mesh axis runs over, the one named last changes fastest.
Arguments:
- table_rows: int32 [9, 262144], P(None, 'dp'), may hold values from 0 to 255
- attribute_order: int32 [9], replicated, may hold values from 0 to 8, each once
- log_potential: float32 [8, 256, 256], P('clique'), may hold values from -4 to 18
- measure_noise: float32 [8, 256, 256], P('clique'), may hold values from -24 to 24
Outputs:
- updated_potentials: float32 [8, 256, 256], P('clique')
- beliefs: float32 [8, 256, 256], P('clique')
The draws below stay inside these ranges and needn't reach their ends.
Inputs may be any that keep to these rules, and one draw needn't show every extreme that they name: `attribute_order`: each of the 9 attributes appears once.
All inputs are finite; a program needn't handle non-finite values.
Results may differ from the reference program's by a relative error of at most 0.0003.
Values sent between devices are 32-bit elements; how exact they have to be, the bound alone decides.
A program may use at most 128 MiB of HBM per device.

```python
import math
import jax
import jax.numpy as jnp
from jax import lax

DOM = 256
CELLS = 65536
ROUNDS = 1
CLIQUES = 8
ATTRS = 9
ROWS = 262144


def draw_log_potential(key, part):
    first_key, second_key, third_key, fourth_key = jax.random.split(key, 4)
    base = 0.7 * jax.random.normal(first_key, (CLIQUES, DOM, DOM), jnp.float32)
    upper = math.log(10.0)
    row_offset = jax.random.uniform(second_key, (CLIQUES, DOM, 1), jnp.float32, 0.0, upper)
    column_offset = jax.random.uniform(third_key, (CLIQUES, 1, DOM), jnp.float32, 0.0, upper)
    shifts = jax.random.randint(fourth_key, (CLIQUES, 1, 1), 0, DOM)
    row_index = jnp.arange(DOM, dtype=jnp.int32)[:, None]
    column_index = jnp.arange(DOM, dtype=jnp.int32)[None, :]
    distance = (column_index - row_index - shifts) % DOM
    band_width = 2
    band = jnp.where(distance < band_width, 9.0, 0.0).astype(jnp.float32)
    return jnp.clip(base, -3.5, 3.5) + row_offset + column_offset + band


def touch_ends(array, stream_key, smallest, largest):
    spot = [jax.random.randint(jax.random.fold_in(stream_key, axis), (), 0, length) for axis, length in enumerate(array.shape)]
    widest = array.shape.index(max(array.shape))
    neighbour = spot[:widest] + [(spot[widest] + 1) % array.shape[widest]] + spot[widest + 1:]
    return array.at[tuple(spot)].set(smallest).at[tuple(neighbour)].set(largest)


def block_levels(stream_key, dims, cuts, low, largest):
    gain, own = 1.0, jax.random.fold_in(stream_key, 6)
    for position, blocks in cuts:
        heights = jnp.exp(jax.random.uniform(jax.random.fold_in(own, position), (blocks,), jnp.float32, low / len(cuts), largest / len(cuts)))
        gain = gain * jnp.repeat(heights, dims[position] // blocks).reshape([-1 if axis == position else 1 for axis in range(len(dims))])
    return gain


def normal_values(stream_key, shape, scale, bound, shards=(), kind=jnp.bfloat16):
    gain = block_levels(stream_key, shape, shards, -0.22, 0.18) if shards else 1.0
    array = jax.random.normal(stream_key, shape, jnp.float32) * scale * gain
    return jnp.minimum(jnp.maximum(array, -bound), bound).astype(kind)


def setup_inputs(seed: int = 0) -> dict:
    seeds = jax.random.split(jax.random.key(seed), 5)
    return {
        "table_rows": touch_ends(jax.random.randint(seeds[0], (ATTRS, ROWS), 0, DOM), jax.random.fold_in(seeds[0], 1), 0, DOM - 1).astype(jnp.int32),
        "attribute_order": jax.random.permutation(seeds[1], ATTRS).astype(jnp.int32),
        "log_potential": draw_log_potential(jax.random.fold_in(seeds[4], 71), 0),
        "measure_noise": normal_values(seeds[3], (CLIQUES, DOM, DOM), 4.0, 24.0, ((0, 8),), jnp.float32),
    }


HIGH = lax.Precision.HIGHEST
step_size = 0.25


def count_pair(table_rows, attribute_pair):
    left = jnp.take(table_rows, attribute_pair[0], axis=0)
    right = jnp.take(table_rows, attribute_pair[1], axis=0)
    cell_ids = (left * DOM + right).astype(jnp.int32)
    tally = jnp.zeros((DOM * DOM,), jnp.float32).at[cell_ids].add(jnp.ones(cell_ids.shape, jnp.float32))
    return tally.reshape(DOM, DOM)


def marginals(potential):
    kernels = jnp.exp(potential)

    def go_forward(carry, kernel):
        moved = jnp.dot(carry, kernel, precision=HIGH)
        return moved / jnp.sum(moved), carry

    def go_backward(carry, kernel):
        moved = jnp.dot(kernel, carry, precision=HIGH)
        return moved / jnp.sum(moved), carry

    all_ones = jnp.ones((DOM,), jnp.float32)
    unused_last, forward = lax.scan(go_forward, all_ones, kernels)
    unused_first, backward = lax.scan(go_backward, all_ones, kernels, reverse=True)
    joint = forward[:, :, None] * kernels * backward[:, None, :]
    total = jnp.sum(joint, axis=(1, 2), keepdims=True)
    return joint * (DOM * DOM) / total


def reference(table_rows, attribute_order, log_potential, measure_noise):
    attribute_pairs = jnp.stack([attribute_order[:-1], attribute_order[1:]], axis=1)

    def count_one(attribute_pair):
        return count_pair(table_rows, attribute_pair)

    counts = lax.map(count_one, attribute_pairs)
    measured = (counts + measure_noise) * (CELLS / ROWS)
    potential = log_potential
    beliefs = potential
    for round_id in range(ROUNDS):
        beliefs = marginals(potential)
        potential = potential - step_size * (beliefs - measured)
    return potential, beliefs
```

```python
import functools
import math

import jax
import jax.numpy as jnp
from jax import lax
from jax.experimental import pallas as pl
from jax.experimental.pallas import tpu as pltpu
from jax.sharding import PartitionSpec as P

step_size = 0.25
PIECES = 4
BLOCK = 2048
QUARTERS = 4
MESH = pl.DeviceIdType.MESH
BF16 = jnp.bfloat16
F32 = jnp.float32


def split_high_low(value):
    high = value.astype(BF16)
    return high, (value - high.astype(F32)).astype(BF16)


def message_rows(vector):
    wide = jnp.broadcast_to(vector, (16, vector.shape[1]))
    high = wide.astype(BF16).astype(F32)
    row = lax.broadcasted_iota(jnp.int32, wide.shape, 0)
    return jnp.where(row < 8, high, wide - high).astype(BF16)


def carry(vector, kernel_high, kernel_low, contract):
    rows = message_rows(vector)
    dims = (((1,), (contract,)), ((), ()))
    moved = lax.dot_general(rows, kernel_high[...], dims, preferred_element_type=F32)
    moved += lax.dot_general(rows, kernel_low[...], dims, preferred_element_type=F32)
    return (moved[0:1] + moved[8:9]) / jnp.sum(vector)


def one_hot(values, domain_size):
    wide = jnp.broadcast_to(values.astype(F32), (16, values.shape[1])).astype(BF16)
    level = lax.broadcasted_iota(jnp.int32, wide.shape, 0).astype(F32)
    tiles = []
    for start in range(0, domain_size, 16):
        hit = wide == (level + float(start)).astype(BF16)
        tiles.append(jnp.where(hit, jnp.ones((), BF16), jnp.zeros((), BF16)))
    return jnp.concatenate(tiles, axis=0)


def kernel(
    sizes, scale, order, table, potential, noise, updated, beliefs,
    tabs, acc, q, q_high, q_low, f_in, f_out, g_in, g_out, sibling, half, across, total,
    tab_sem, f_sem, g_sem, send1, recv1, send2, recv2, send3, recv3,
):
    cliques, copies = sizes
    domain = q.shape[0]
    columns = tabs[0].shape[1]
    blocks = columns // BLOCK
    chips = copies // 2
    rows = domain // 2 // PIECES
    k = lax.axis_index("clique")
    d = lax.axis_index("dp")
    chip, core = d // 2, lax.rem(d, 2)
    twin = chip * 2 + 1 - core

    loads = []
    for quarter, tab in enumerate(tabs):
        where = pl.ds(quarter * columns, columns)
        load = pltpu.make_async_copy(table.at[:, where], tab, tab_sem.at[quarter])
        load.start()
        loads.append(load)

    barrier = pltpu.get_barrier_semaphore()

    def greet(device):
        pl.semaphore_signal(barrier, inc=1, device_id=device, device_id_type=MESH)

    greet({"dp": twin})
    for step in range(1, chips):
        greet({"dp": lax.rem(chip + step, chips) * 2 + core})

    @pl.when(k > 0)
    def _():
        greet({"clique": k - 1})

    @pl.when(k < cliques - 1)
    def _():
        greet({"clique": k + 1})

    q[...] = jnp.exp(potential[...])
    q_high[...], q_low[...] = split_high_low(q[...])
    acc[...] = jnp.zeros_like(acc)

    @pl.when(k == 0)
    def _():
        f_in[...] = jnp.ones_like(f_in)

    @pl.when(k == cliques - 1)
    def _():
        g_in[...] = jnp.ones_like(g_in)

    at_end = jnp.logical_or(k == 0, k == cliques - 1)

    @pl.when(at_end)
    def _():
        pl.semaphore_wait(barrier, chips + 1)

    @pl.when(jnp.logical_not(at_end))
    def _():
        pl.semaphore_wait(barrier, chips + 2)

    f_copy = pltpu.make_async_remote_copy(
        f_out, f_in, f_sem.at[0], f_sem.at[1], {"clique": lax.rem(k + 1, cliques)}, MESH
    )
    g_copy = pltpu.make_async_remote_copy(
        g_out, g_in, g_sem.at[0], g_sem.at[1],
        {"clique": lax.rem(k + cliques - 1, cliques)}, MESH,
    )

    def forward():
        @pl.when(k > 0)
        def _():
            f_copy.wait_recv()

        @pl.when(k < cliques - 1)
        def _():
            f_out[...] = carry(f_in[...], q_high, q_low, 0)
            f_copy.start()

    def backward():
        @pl.when(k < cliques - 1)
        def _():
            g_copy.wait_recv()

        @pl.when(k > 0)
        def _():
            g_out[...] = carry(g_in[...], q_high, q_low, 1)
            g_copy.start()

    left, right = order[k], order[k + 1]
    per = max(1, QUARTERS * blocks // cliques)

    for quarter, tab in enumerate(tabs):
        loads[quarter].wait()

        @pl.loop(0, blocks)
        def _(block, tab=tab, quarter=quarter):
            where = pl.ds(pl.multiple_of(block * BLOCK, BLOCK), BLOCK)
            first = one_hot(tab[pl.ds(left, 1), where], domain)
            second = one_hot(tab[pl.ds(right, 1), where], domain)
            acc[...] += lax.dot_general(
                first, second, (((1,), (1,)), ((), ())), preferred_element_type=F32
            )
            done = quarter * blocks + block
            pl.when(done == k * per)(forward)
            pl.when(done == (cliques - 1 - k) * per)(backward)

    for late in range(QUARTERS * blocks, cliques):
        pl.when(k == late)(forward)
        pl.when(cliques - 1 - k == late)(backward)

    mine, theirs = core * (domain // 2), (1 - core) * (domain // 2)

    def part(base, piece):
        return pl.ds(pl.multiple_of(base + piece * rows, rows), rows)

    first_trip, second_trip, third_trip = [], [], []
    for piece in range(PIECES):
        copy = pltpu.make_async_remote_copy(
            acc.at[part(theirs, piece)], sibling.at[piece],
            send1.at[piece], recv1.at[piece], {"dp": twin}, MESH,
        )
        copy.start()
        first_trip.append(copy)
    for piece in range(PIECES):
        first_trip[piece].wait_recv()
        half[piece] = acc[part(mine, piece), :] + sibling[piece]
        for step in range(1, chips):
            copy = pltpu.make_async_remote_copy(
                half.at[piece], across.at[step - 1, piece],
                send2.at[step - 1, piece], recv2.at[step - 1, piece],
                {"dp": lax.rem(chip + step, chips) * 2 + core}, MESH,
            )
            copy.start()
            second_trip.append(copy)

    column = jnp.transpose(jnp.broadcast_to(f_in[...], (8, domain)))[:, 0:1]
    joint = (column / jnp.sum(f_in[...])) * q[...] * (g_in[...] / jnp.sum(g_in[...]))
    beliefs[...] = joint * (float(domain * domain) / jnp.sum(joint))

    def finish(where):
        measured = (total[where, :] + noise[where, :]) * scale
        updated[where, :] = potential[where, :] - step_size * (beliefs[where, :] - measured)

    for piece in range(PIECES):
        summed = half[piece]
        for step in range(1, chips):
            second_trip[piece * (chips - 1) + step - 1].wait_recv()
            summed = summed + across[step - 1, piece]
        total[part(mine, piece), :] = summed
        copy = pltpu.make_async_remote_copy(
            total.at[part(mine, piece)], total.at[part(mine, piece)],
            send3.at[piece], recv3.at[piece], {"dp": twin}, MESH,
        )
        copy.start()
        third_trip.append(copy)
        finish(part(mine, piece))
    for piece in range(PIECES):
        third_trip[piece].wait_recv()
        finish(part(theirs, piece))

    for copy in first_trip + second_trip + third_trip:
        copy.wait_send()

    @pl.when(k < cliques - 1)
    def _():
        f_copy.wait_send()

    @pl.when(k > 0)
    def _():
        g_copy.wait_send()


def per_device(table_rows, attribute_order, log_potential, measure_noise):
    cliques, copies = lax.axis_size("clique"), lax.axis_size("dp")
    domain = log_potential.shape[1]
    attributes, columns = table_rows.shape
    scale = domain * domain / (columns * copies)
    rows = domain // 2 // PIECES
    chips = copies // 2
    table = jax.ShapeDtypeStruct((domain, domain), F32)
    vmem = pl.BlockSpec(memory_space=pltpu.VMEM)
    dma = pltpu.SemaphoreType.DMA
    updated, beliefs = pl.pallas_call(
        functools.partial(kernel, (cliques, copies), scale),
        out_shape=(table, table),
        in_specs=[
            pl.BlockSpec(memory_space=pltpu.SMEM),
            pl.BlockSpec(memory_space=pl.ANY),
            vmem,
            vmem,
        ],
        out_specs=(vmem, vmem),
        scratch_shapes=[
            [pltpu.VMEM((attributes, columns // QUARTERS), jnp.int32)] * QUARTERS,
            pltpu.VMEM((domain, domain), F32),
            pltpu.VMEM((domain, domain), F32),
            pltpu.VMEM((domain, domain), BF16),
            pltpu.VMEM((domain, domain), BF16),
            pltpu.VMEM((1, domain), F32),
            pltpu.VMEM((1, domain), F32),
            pltpu.VMEM((1, domain), F32),
            pltpu.VMEM((1, domain), F32),
            pltpu.VMEM((PIECES, rows, domain), F32),
            pltpu.VMEM((PIECES, rows, domain), F32),
            pltpu.VMEM((chips - 1, PIECES, rows, domain), F32),
            pltpu.VMEM((domain, domain), F32),
            dma((QUARTERS,)),
            dma((2,)),
            dma((2,)),
            dma((PIECES,)),
            dma((PIECES,)),
            dma((chips - 1, PIECES)),
            dma((chips - 1, PIECES)),
            dma((PIECES,)),
            dma((PIECES,)),
        ],
        compiler_params=pltpu.CompilerParams(
            collective_id=0, has_side_effects=True, vmem_limit_bytes=48 * 1024 * 1024
        ),
    )(attribute_order, table_rows, log_potential[0], measure_noise[0])
    return updated[None], beliefs[None]


def solution(mesh):
    in_specs = (P(None, "dp"), P(), P("clique", None, None), P("clique", None, None))
    out_specs = (P("clique", None, None), P("clique", None, None))
    return jax.shard_map(
        per_device, mesh=mesh, in_specs=in_specs, out_specs=out_specs, check_vma=False
    )
```

```python
import functools
import math

import jax
import jax.numpy as jnp
from jax import lax
from jax.experimental import pallas as pl
from jax.experimental.pallas import tpu as pltpu
from jax.sharding import PartitionSpec as P

step_size = 0.25
PIECES = 4
BLOCK = 2048
QUARTERS = 4
MESH = pl.DeviceIdType.MESH
BF16 = jnp.bfloat16
F32 = jnp.float32
ONE = jnp.float8_e4m3fn


def split_high_low(value):
    high = value.astype(BF16)
    return high, (value - high.astype(F32)).astype(BF16)


def message_rows(vector):
    wide = jnp.broadcast_to(vector, (16, vector.shape[1]))
    high = wide.astype(BF16).astype(F32)
    row = lax.broadcasted_iota(jnp.int32, wide.shape, 0)
    return jnp.where(row < 8, high, wide - high).astype(BF16)


def carry(vector, kernel_high, kernel_low, contract):
    rows = message_rows(vector)
    dims = (((1,), (contract,)), ((), ()))
    moved = lax.dot_general(rows, kernel_high[...], dims, preferred_element_type=F32)
    moved += lax.dot_general(rows, kernel_low[...], dims, preferred_element_type=F32)
    return (moved[0:1] + moved[8:9]) / jnp.sum(vector)


def fill_one_hot(tab, attribute, start, levels, slot):
    kinds, deep, lanes = levels.shape
    width = slot.shape[1]
    values = tab[pl.ds(attribute, 1), pl.ds(pl.multiple_of(start, width), width)] - 128
    for tile in range(0, width, lanes):
        wide = jnp.broadcast_to(values[:, tile : tile + lanes], (deep, lanes))
        hit = wide.astype(jnp.int8)[None] == levels
        ones = jnp.where(hit, jnp.ones((), ONE), jnp.zeros((), ONE))
        slot[:, tile : tile + lanes] = ones.reshape(kinds * deep, lanes)


def kernel(
    sizes, scale, order, table, potential_in, noise_in, updated, beliefs,
    tabs, slots, potential, noise, acc, q, q_high, q_low, f_in, f_out, g_in, g_out, sibling, half, across, total,
    tab_sem, in_sem, f_sem, g_sem, send1, recv1, send2, recv2, send3, recv3,
):
    cliques, copies = sizes
    domain = q.shape[0]
    columns = tabs[0].shape[1]
    blocks = columns // BLOCK
    chips = copies // 2
    rows = domain // 2 // PIECES
    k = lax.axis_index("clique")
    d = lax.axis_index("dp")
    chip, core = d // 2, lax.rem(d, 2)
    twin = chip * 2 + 1 - core

    get_potential = pltpu.make_async_copy(potential_in.at[0], potential, in_sem.at[0])
    get_potential.start()
    loads = []
    for quarter, tab in enumerate(tabs):
        where = pl.ds(quarter * columns, columns)
        load = pltpu.make_async_copy(table.at[:, where], tab, tab_sem.at[quarter])
        load.start()
        loads.append(load)
    get_noise = pltpu.make_async_copy(noise_in.at[0], noise, in_sem.at[1])
    get_noise.start()

    barrier = pltpu.get_barrier_semaphore()

    def greet(device):
        pl.semaphore_signal(barrier, inc=1, device_id=device, device_id_type=MESH)

    greet({"dp": twin})
    for step in range(1, chips):
        greet({"dp": lax.rem(chip + step, chips) * 2 + core})

    @pl.when(k > 0)
    def _():
        greet({"clique": k - 1})

    @pl.when(k < cliques - 1)
    def _():
        greet({"clique": k + 1})

    get_potential.wait()
    q[...] = jnp.exp(potential[...])
    q_high[...], q_low[...] = split_high_low(q[...])
    acc[...] = jnp.zeros_like(acc)
    slots[1][0][...] = jnp.zeros_like(slots[1][0])
    slots[1][1][...] = jnp.zeros_like(slots[1][1])

    @pl.when(k == 0)
    def _():
        f_in[...] = jnp.ones_like(f_in)

    @pl.when(k == cliques - 1)
    def _():
        g_in[...] = jnp.ones_like(g_in)

    at_end = jnp.logical_or(k == 0, k == cliques - 1)

    @pl.when(at_end)
    def _():
        pl.semaphore_wait(barrier, chips + 1)

    @pl.when(jnp.logical_not(at_end))
    def _():
        pl.semaphore_wait(barrier, chips + 2)

    f_copy = pltpu.make_async_remote_copy(
        f_out, f_in, f_sem.at[0], f_sem.at[1], {"clique": lax.rem(k + 1, cliques)}, MESH
    )
    g_copy = pltpu.make_async_remote_copy(
        g_out, g_in, g_sem.at[0], g_sem.at[1],
        {"clique": lax.rem(k + cliques - 1, cliques)}, MESH,
    )

    def forward():
        @pl.when(k > 0)
        def _():
            f_copy.wait_recv()

        @pl.when(k < cliques - 1)
        def _():
            f_out[...] = carry(f_in[...], q_high, q_low, 0)
            f_copy.start()

    def backward():
        @pl.when(k < cliques - 1)
        def _():
            g_copy.wait_recv()

        @pl.when(k > 0)
        def _():
            g_out[...] = carry(g_in[...], q_high, q_low, 1)
            g_copy.start()

    left, right = order[k], order[k + 1]
    pairs = blocks // 2
    per = max(1, QUARTERS * pairs // cliques)
    shape = (domain // 32, 32, 128)
    level = lax.broadcasted_iota(jnp.int32, shape, 0) * 32
    level += lax.broadcasted_iota(jnp.int32, shape, 1)
    levels = (level - 128).astype(jnp.int8)

    def multiply(slot):
        acc[...] += lax.dot_general(
            slot[0][...], slot[1][...], (((1,), (1,)), ((), ())),
            preferred_element_type=F32,
        )

    for quarter, tab in enumerate(tabs):
        loads[quarter].wait()

        @pl.loop(0, pairs)
        def _(pair, tab=tab, quarter=quarter):
            for turn in range(2):
                start = (pair * 2 + turn) * BLOCK
                fill_one_hot(tab, left, start, levels, slots[turn][0])
                fill_one_hot(tab, right, start, levels, slots[turn][1])
                multiply(slots[1 - turn])
            done = quarter * pairs + pair
            pl.when(done == k * per)(forward)
            pl.when(done == (cliques - 1 - k) * per)(backward)

    multiply(slots[1])
    for late in range(QUARTERS * pairs, cliques):
        pl.when(k == late)(forward)
        pl.when(cliques - 1 - k == late)(backward)

    mine, theirs = core * (domain // 2), (1 - core) * (domain // 2)

    def part(base, piece):
        return pl.ds(pl.multiple_of(base + piece * rows, rows), rows)

    first_trip, second_trip, third_trip = [], [], []
    for piece in range(PIECES):
        copy = pltpu.make_async_remote_copy(
            acc.at[part(theirs, piece)], sibling.at[piece],
            send1.at[piece], recv1.at[piece], {"dp": twin}, MESH,
        )
        copy.start()
        first_trip.append(copy)
    for piece in range(PIECES):
        first_trip[piece].wait_recv()
        half[piece] = acc[part(mine, piece), :] + sibling[piece]
        for step in range(1, chips):
            copy = pltpu.make_async_remote_copy(
                half.at[piece], across.at[step - 1, piece],
                send2.at[step - 1, piece], recv2.at[step - 1, piece],
                {"dp": lax.rem(chip + step, chips) * 2 + core}, MESH,
            )
            copy.start()
            second_trip.append(copy)

    column = jnp.transpose(jnp.broadcast_to(f_in[...], (8, domain)))[:, 0:1]
    joint = (column / jnp.sum(f_in[...])) * q[...] * (g_in[...] / jnp.sum(g_in[...]))
    beliefs[...] = joint * (float(domain * domain) / jnp.sum(joint))

    get_noise.wait()

    def finish(where):
        measured = (total[where, :] + noise[where, :]) * scale
        updated[where, :] = potential[where, :] - step_size * (beliefs[where, :] - measured)

    for piece in range(PIECES):
        summed = half[piece]
        for step in range(1, chips):
            second_trip[piece * (chips - 1) + step - 1].wait_recv()
            summed = summed + across[step - 1, piece]
        total[part(mine, piece), :] = summed
        copy = pltpu.make_async_remote_copy(
            total.at[part(mine, piece)], total.at[part(mine, piece)],
            send3.at[piece], recv3.at[piece], {"dp": twin}, MESH,
        )
        copy.start()
        third_trip.append(copy)
        finish(part(mine, piece))
    for piece in range(PIECES):
        third_trip[piece].wait_recv()
        finish(part(theirs, piece))

    for copy in first_trip + second_trip + third_trip:
        copy.wait_send()

    @pl.when(k < cliques - 1)
    def _():
        f_copy.wait_send()

    @pl.when(k > 0)
    def _():
        g_copy.wait_send()


def per_device(table_rows, attribute_order, log_potential, measure_noise):
    cliques, copies = lax.axis_size("clique"), lax.axis_size("dp")
    domain = log_potential.shape[1]
    attributes, columns = table_rows.shape
    scale = domain * domain / (columns * copies)
    rows = domain // 2 // PIECES
    chips = copies // 2
    table = jax.ShapeDtypeStruct((domain, domain), F32)
    vmem = pl.BlockSpec(memory_space=pltpu.VMEM)
    hbm = pl.BlockSpec(memory_space=pl.ANY)
    dma = pltpu.SemaphoreType.DMA
    updated, beliefs = pl.pallas_call(
        functools.partial(kernel, (cliques, copies), scale),
        out_shape=(table, table),
        in_specs=[
            pl.BlockSpec(memory_space=pltpu.SMEM),
            hbm,
            hbm,
            hbm,
        ],
        out_specs=(vmem, vmem),
        scratch_shapes=[
            [pltpu.VMEM((attributes, columns // QUARTERS), jnp.int32)] * QUARTERS,
            [[pltpu.VMEM((domain, BLOCK), ONE)] * 2] * 2,
            pltpu.VMEM((domain, domain), F32),
            pltpu.VMEM((domain, domain), F32),
            pltpu.VMEM((domain, domain), F32),
            pltpu.VMEM((domain, domain), F32),
            pltpu.VMEM((domain, domain), BF16),
            pltpu.VMEM((domain, domain), BF16),
            pltpu.VMEM((1, domain), F32),
            pltpu.VMEM((1, domain), F32),
            pltpu.VMEM((1, domain), F32),
            pltpu.VMEM((1, domain), F32),
            pltpu.VMEM((PIECES, rows, domain), F32),
            pltpu.VMEM((PIECES, rows, domain), F32),
            pltpu.VMEM((chips - 1, PIECES, rows, domain), F32),
            pltpu.VMEM((domain, domain), F32),
            dma((QUARTERS,)),
            dma((2,)),
            dma((2,)),
            dma((2,)),
            dma((PIECES,)),
            dma((PIECES,)),
            dma((chips - 1, PIECES)),
            dma((chips - 1, PIECES)),
            dma((PIECES,)),
            dma((PIECES,)),
        ],
        compiler_params=pltpu.CompilerParams(
            collective_id=0, has_side_effects=True, vmem_limit_bytes=60 * 1024 * 1024
        ),
    )(attribute_order, table_rows, log_potential, measure_noise)
    return updated[None], beliefs[None]


def solution(mesh):
    in_specs = (P(None, "dp"), P(), P("clique", None, None), P("clique", None, None))
    out_specs = (P("clique", None, None), P("clique", None, None))
    return jax.shard_map(
        per_device, mesh=mesh, in_specs=in_specs, out_specs=out_specs, check_vma=False
    )
```

```python
import functools
import math

import jax
import jax.numpy as jnp
from jax import lax
from jax.experimental import pallas as pl
from jax.experimental.pallas import tpu as pltpu
from jax.sharding import PartitionSpec as P

step_size = 0.25
PIECES = 4
BLOCK = 2048
QUARTERS = 4
MEET = 9
MESH = pl.DeviceIdType.MESH
BF16 = jnp.bfloat16
F32 = jnp.float32
ONE = jnp.float8_e4m3fn


def split_high_low(value):
    high = value.astype(BF16)
    return high, (value - high.astype(F32)).astype(BF16)


def message_rows(vector):
    wide = jnp.broadcast_to(vector, (16, vector.shape[1]))
    high = wide.astype(BF16).astype(F32)
    row = lax.broadcasted_iota(jnp.int32, wide.shape, 0)
    return jnp.where(row < 8, high, wide - high).astype(BF16)


def carry(vector, kernel_high, kernel_low, contract):
    rows = message_rows(vector)
    dims = (((1,), (contract,)), ((), ()))
    moved = lax.dot_general(rows, kernel_high[...], dims, preferred_element_type=F32)
    moved += lax.dot_general(rows, kernel_low[...], dims, preferred_element_type=F32)
    return (moved[0:1] + moved[8:9]) / jnp.sum(vector)


def fill_one_hot(tab, attribute, start, levels, slot):
    kinds, deep, lanes = levels.shape
    width = slot.shape[1]
    values = tab[pl.ds(attribute, 1), pl.ds(pl.multiple_of(start, width), width)] - 128
    for tile in range(0, width, lanes):
        wide = jnp.broadcast_to(values[:, tile : tile + lanes], (deep, lanes))
        hit = wide.astype(jnp.int8)[None] == levels
        ones = jnp.where(hit, jnp.ones((), ONE), jnp.zeros((), ONE))
        slot[:, tile : tile + lanes] = ones.reshape(kinds * deep, lanes)


def kernel(
    sizes, scale, order, table, potential_in, noise_in, updated, beliefs,
    tabs, slots, potential, noise, acc, q, q_high, q_low, m_high, m_low,
    vectors, sibling, half, across, total,
    tab_sem, in_sem, pair_sem, f_sem, g_sem, send1, recv1, send2, recv2, send3, recv3,
):
    cliques, copies = sizes
    f_in, f_out, g_in, g_out, f_own, g_own = vectors
    domain = acc.shape[0]
    groups = cliques // 2
    columns = tabs[0].shape[1]
    blocks = columns // BLOCK
    chips = copies // 2
    rows = domain // 2 // PIECES
    k = lax.axis_index("clique")
    d = lax.axis_index("dp")
    chip, core = d // 2, lax.rem(d, 2)
    twin = chip * 2 + 1 - core
    group, odd = k // 2, lax.rem(k, 2)
    partner = group * 2 + 1 - odd

    get_potential = pltpu.make_async_copy(
        potential_in.at[0], potential.at[odd], in_sem.at[0]
    )
    get_potential.start()
    loads = []
    for quarter, tab in enumerate(tabs):
        where = pl.ds(quarter * columns, columns)
        load = pltpu.make_async_copy(table.at[:, where], tab, tab_sem.at[quarter])
        load.start()
        loads.append(load)
    get_noise = pltpu.make_async_copy(noise_in.at[0], noise, in_sem.at[1])
    get_noise.start()

    barrier = pltpu.get_barrier_semaphore()

    def greet(device):
        pl.semaphore_signal(barrier, inc=1, device_id=device, device_id_type=MESH)

    greet({"dp": twin})
    for step in range(1, chips):
        greet({"dp": lax.rem(chip + step, chips) * 2 + core})

    greet({"clique": partner})

    @pl.when(group > 0)
    def _():
        greet({"clique": k - 2})

    @pl.when(group < groups - 1)
    def _():
        greet({"clique": k + 2})

    acc[...] = jnp.zeros_like(acc)
    slots[1][0][...] = jnp.zeros_like(slots[1][0])
    slots[1][1][...] = jnp.zeros_like(slots[1][1])

    @pl.when(group == 0)
    def _():
        f_in[...] = jnp.ones_like(f_in)

    @pl.when(group == groups - 1)
    def _():
        g_in[...] = jnp.ones_like(g_in)

    at_end = jnp.logical_or(group == 0, group == groups - 1)

    @pl.when(at_end)
    def _():
        pl.semaphore_wait(barrier, chips + 2)

    @pl.when(jnp.logical_not(at_end))
    def _():
        pl.semaphore_wait(barrier, chips + 3)

    pair_copy = pltpu.make_async_remote_copy(
        potential_in.at[0], potential.at[odd], pair_sem.at[0], pair_sem.at[1],
        {"clique": partner}, MESH,
    )
    pair_copy.start()
    f_copy = pltpu.make_async_remote_copy(
        f_out, f_in, f_sem.at[0], f_sem.at[1], {"clique": lax.rem(k + 2, cliques)}, MESH
    )
    g_copy = pltpu.make_async_remote_copy(
        g_out, g_in, g_sem.at[0], g_sem.at[1],
        {"clique": lax.rem(k + cliques - 2, cliques)}, MESH,
    )

    def prepare(which):
        q[which] = jnp.exp(potential[which])
        q_high[which], q_low[which] = split_high_low(q[which])

    get_potential.wait()
    prepare(odd)

    def pair_product():
        pair_copy.wait_recv()
        prepare(1 - odd)
        product = jnp.dot(q_high[0], q_high[1], preferred_element_type=F32)
        product += jnp.dot(q_high[0], q_low[1], preferred_element_type=F32)
        product += jnp.dot(q_low[0], q_high[1], preferred_element_type=F32)
        m_high[...], m_low[...] = split_high_low(product)

    def stage(number):
        @pl.when(group == number)
        def _():
            if number > 0:
                f_copy.wait_recv()
            if number < groups - 1:
                f_out[...] = carry(f_in[...], m_high, m_low, 0)
                f_copy.start()

        @pl.when(group == groups - 1 - number)
        def _():
            if number > 0:
                g_copy.wait_recv()
            if number < groups - 1:
                g_out[...] = carry(g_in[...], m_high, m_low, 1)
                g_copy.start()

    left, right = order[k], order[k + 1]
    pairs = blocks // 2
    meet = min(MEET, QUARTERS * pairs - 1)
    shape = (domain // 32, 32, 128)
    level = lax.broadcasted_iota(jnp.int32, shape, 0) * 32
    level += lax.broadcasted_iota(jnp.int32, shape, 1)
    levels = (level - 128).astype(jnp.int8)

    def multiply(slot):
        acc[...] += lax.dot_general(
            slot[0][...], slot[1][...], (((1,), (1,)), ((), ())),
            preferred_element_type=F32,
        )

    for quarter, tab in enumerate(tabs):
        loads[quarter].wait()

        @pl.loop(0, pairs)
        def _(pair, tab=tab, quarter=quarter):
            for turn in range(2):
                start = (pair * 2 + turn) * BLOCK
                fill_one_hot(tab, left, start, levels, slots[turn][0])
                fill_one_hot(tab, right, start, levels, slots[turn][1])
                multiply(slots[1 - turn])

            @pl.when(quarter * pairs + pair == meet)
            def _():
                pair_product()
                stage(0)

    multiply(slots[1])
    mine, theirs = core * (domain // 2), (1 - core) * (domain // 2)

    def part(base, piece):
        return pl.ds(pl.multiple_of(base + piece * rows, rows), rows)

    first_trip, second_trip, third_trip = [], [], []
    for piece in range(PIECES):
        copy = pltpu.make_async_remote_copy(
            acc.at[part(theirs, piece)], sibling.at[piece],
            send1.at[piece], recv1.at[piece], {"dp": twin}, MESH,
        )
        copy.start()
        first_trip.append(copy)
    for number in range(1, groups - 2):
        stage(number)
    for piece in range(PIECES):
        first_trip[piece].wait_recv()
        half[piece] = acc[part(mine, piece), :] + sibling[piece]
        for step in range(1, chips):
            copy = pltpu.make_async_remote_copy(
                half.at[piece], across.at[step - 1, piece],
                send2.at[step - 1, piece], recv2.at[step - 1, piece],
                {"dp": lax.rem(chip + step, chips) * 2 + core}, MESH,
            )
            copy.start()
            second_trip.append(copy)

    for number in range(max(1, groups - 2), groups - 1):
        stage(number)
    get_noise.wait()

    for piece in range(PIECES):
        summed = half[piece]
        for step in range(1, chips):
            second_trip[piece * (chips - 1) + step - 1].wait_recv()
            summed = summed + across[step - 1, piece]
        total[part(mine, piece), :] = summed
        copy = pltpu.make_async_remote_copy(
            total.at[part(mine, piece)], total.at[part(mine, piece)],
            send3.at[piece], recv3.at[piece], {"dp": twin}, MESH,
        )
        copy.start()
        third_trip.append(copy)

    if groups > 1:
        stage(groups - 1)

    @pl.when(odd == 1)
    def _():
        f_own[...] = carry(f_in[...], q_high.at[0], q_low.at[0], 0)
        g_own[...] = g_in[...]

    @pl.when(odd == 0)
    def _():
        f_own[...] = f_in[...]
        g_own[...] = carry(g_in[...], q_high.at[1], q_low.at[1], 1)

    f, g = f_own[...], g_own[...]
    column = jnp.transpose(jnp.broadcast_to(f / jnp.sum(f), (8, domain)))[:, 0:1]
    joint = column * q[odd] * (g / jnp.sum(g))
    beliefs[...] = joint * (float(domain * domain) / jnp.sum(joint))

    def finish(where):
        measured = (total[where, :] + noise[where, :]) * scale
        updated[where, :] = potential[odd, where, :] - step_size * (beliefs[where, :] - measured)

    for piece in range(PIECES):
        finish(part(mine, piece))
    for piece in range(PIECES):
        third_trip[piece].wait_recv()
        finish(part(theirs, piece))

    for copy in first_trip + second_trip + third_trip:
        copy.wait_send()

    pair_copy.wait_send()

    @pl.when(group < groups - 1)
    def _():
        f_copy.wait_send()

    @pl.when(group > 0)
    def _():
        g_copy.wait_send()


def per_device(table_rows, attribute_order, log_potential, measure_noise):
    cliques, copies = lax.axis_size("clique"), lax.axis_size("dp")
    domain = log_potential.shape[1]
    attributes, columns = table_rows.shape
    scale = domain * domain / (columns * copies)
    rows = domain // 2 // PIECES
    chips = copies // 2
    table = jax.ShapeDtypeStruct((domain, domain), F32)
    vmem = pl.BlockSpec(memory_space=pltpu.VMEM)
    hbm = pl.BlockSpec(memory_space=pl.ANY)
    dma = pltpu.SemaphoreType.DMA
    updated, beliefs = pl.pallas_call(
        functools.partial(kernel, (cliques, copies), scale),
        out_shape=(table, table),
        in_specs=[
            pl.BlockSpec(memory_space=pltpu.SMEM),
            hbm,
            hbm,
            hbm,
        ],
        out_specs=(vmem, vmem),
        scratch_shapes=[
            [pltpu.VMEM((attributes, columns // QUARTERS), jnp.int32)] * QUARTERS,
            [[pltpu.VMEM((domain, BLOCK), ONE)] * 2] * 2,
            pltpu.VMEM((2, domain, domain), F32),
            pltpu.VMEM((domain, domain), F32),
            pltpu.VMEM((domain, domain), F32),
            pltpu.VMEM((2, domain, domain), F32),
            pltpu.VMEM((2, domain, domain), BF16),
            pltpu.VMEM((2, domain, domain), BF16),
            pltpu.VMEM((domain, domain), BF16),
            pltpu.VMEM((domain, domain), BF16),
            [pltpu.VMEM((1, domain), F32)] * 6,
            pltpu.VMEM((PIECES, rows, domain), F32),
            pltpu.VMEM((PIECES, rows, domain), F32),
            pltpu.VMEM((chips - 1, PIECES, rows, domain), F32),
            pltpu.VMEM((domain, domain), F32),
            dma((QUARTERS,)),
            dma((2,)),
            dma((2,)),
            dma((2,)),
            dma((2,)),
            dma((PIECES,)),
            dma((PIECES,)),
            dma((chips - 1, PIECES)),
            dma((chips - 1, PIECES)),
            dma((PIECES,)),
            dma((PIECES,)),
        ],
        compiler_params=pltpu.CompilerParams(
            collective_id=0, has_side_effects=True, vmem_limit_bytes=60 * 1024 * 1024
        ),
    )(attribute_order, table_rows, log_potential, measure_noise)
    return updated[None], beliefs[None]


def solution(mesh):
    in_specs = (P(None, "dp"), P(), P("clique", None, None), P("clique", None, None))
    out_specs = (P("clique", None, None), P("clique", None, None))
    return jax.shard_map(
        per_device, mesh=mesh, in_specs=in_specs, out_specs=out_specs, check_vma=False
    )
```

```python
import functools
import math

import jax
import jax.numpy as jnp
from jax import lax
from jax.experimental import pallas as pl
from jax.experimental.pallas import tpu as pltpu
from jax.sharding import PartitionSpec as P

step_size = 0.25
PIECES = 4
BLOCK = 4096
QUARTERS = 4
MEET = 4
VMEM_LIMIT = 60 * 1024 * 1024
MESH = pl.DeviceIdType.MESH
BF16 = jnp.bfloat16
F32 = jnp.float32
ONE = jnp.float8_e4m3fn


def split_high_low(value):
    high = value.astype(BF16)
    return high, (value - high.astype(F32)).astype(BF16)


def message_rows(vector):
    wide = jnp.broadcast_to(vector, (16, vector.shape[1]))
    high = wide.astype(BF16).astype(F32)
    row = lax.broadcasted_iota(jnp.int32, wide.shape, 0)
    return jnp.where(row < 8, high, wide - high).astype(BF16)


def carry(vector, kernel_high, kernel_low, contract):
    rows = message_rows(vector)
    dims = (((1,), (contract,)), ((), ()))
    moved = lax.dot_general(rows, kernel_high[...], dims, preferred_element_type=F32)
    moved += lax.dot_general(rows, kernel_low[...], dims, preferred_element_type=F32)
    return (moved[0:1] + moved[8:9]) / jnp.sum(vector)


def fill_one_hot(tab, attribute, start, levels, slot):
    kinds, deep, lanes = levels.shape
    width = slot.shape[1]
    values = tab[pl.ds(attribute, 1), pl.ds(pl.multiple_of(start, width), width)] - 128
    for tile in range(0, width, lanes):
        wide = jnp.broadcast_to(values[:, tile : tile + lanes], (deep, lanes))
        hit = wide.astype(jnp.int8)[None] == levels
        ones = jnp.where(hit, jnp.ones((), ONE), jnp.zeros((), ONE))
        slot[:, tile : tile + lanes] = ones.reshape(kinds * deep, lanes)


def kernel(
    sizes, scale, order, table, potential_in, noise_in, updated_out, beliefs_out,
    tabs, slots, potential, noise, updated, beliefs, acc, q, q_high, q_low, m_high, m_low,
    vectors, sibling, half, across, total,
    tab_sem, in_sem, out_sem, pair_sem, f_sem, g_sem, send1, recv1, send2, recv2, send3, recv3,
):
    cliques, copies = sizes
    f_in, f_out, g_in, g_out, f_own, g_own = vectors
    domain = acc.shape[0]
    groups = cliques // 2
    columns = tabs[0].shape[1]
    blocks = columns // BLOCK
    chips = copies // 2
    rows = domain // 2 // PIECES
    k = lax.axis_index("clique")
    d = lax.axis_index("dp")
    chip, core = d // 2, lax.rem(d, 2)
    twin = chip * 2 + 1 - core
    group, odd = k // 2, lax.rem(k, 2)
    partner = group * 2 + 1 - odd

    get_potential = pltpu.make_async_copy(
        potential_in.at[0], potential.at[odd], in_sem.at[0]
    )
    get_potential.start()
    loads = []
    for quarter, tab in enumerate(tabs):
        where = pl.ds(quarter * columns, columns)
        load = pltpu.make_async_copy(table.at[:, where], tab, tab_sem.at[quarter])
        load.start()
        loads.append(load)
    get_noise = pltpu.make_async_copy(noise_in.at[0], noise, in_sem.at[1])
    get_noise.start()

    barrier = pltpu.get_barrier_semaphore()

    def greet(device):
        pl.semaphore_signal(barrier, inc=1, device_id=device, device_id_type=MESH)

    greet({"dp": twin})
    for step in range(1, chips):
        greet({"dp": lax.rem(chip + step, chips) * 2 + core})

    greet({"clique": partner})

    @pl.when(group > 0)
    def _():
        greet({"clique": k - 2})

    @pl.when(group < groups - 1)
    def _():
        greet({"clique": k + 2})

    acc[...] = jnp.zeros_like(acc)
    slots[1][0][...] = jnp.zeros_like(slots[1][0])
    slots[1][1][...] = jnp.zeros_like(slots[1][1])

    @pl.when(group == 0)
    def _():
        f_in[...] = jnp.ones_like(f_in)

    @pl.when(group == groups - 1)
    def _():
        g_in[...] = jnp.ones_like(g_in)

    at_end = jnp.logical_or(group == 0, group == groups - 1)

    @pl.when(at_end)
    def _():
        pl.semaphore_wait(barrier, chips + 2)

    @pl.when(jnp.logical_not(at_end))
    def _():
        pl.semaphore_wait(barrier, chips + 3)

    pair_copy = pltpu.make_async_remote_copy(
        potential_in.at[0], potential.at[odd], pair_sem.at[0], pair_sem.at[1],
        {"clique": partner}, MESH,
    )
    pair_copy.start()
    f_copy = pltpu.make_async_remote_copy(
        f_out, f_in, f_sem.at[0], f_sem.at[1], {"clique": lax.rem(k + 2, cliques)}, MESH
    )
    g_copy = pltpu.make_async_remote_copy(
        g_out, g_in, g_sem.at[0], g_sem.at[1],
        {"clique": lax.rem(k + cliques - 2, cliques)}, MESH,
    )

    def prepare(which):
        q[which] = jnp.exp(potential[which])
        q_high[which], q_low[which] = split_high_low(q[which])

    get_potential.wait()
    prepare(odd)

    def pair_product():
        pair_copy.wait_recv()
        prepare(1 - odd)
        product = jnp.dot(q_high[0], q_high[1], preferred_element_type=F32)
        product += jnp.dot(q_high[0], q_low[1], preferred_element_type=F32)
        product += jnp.dot(q_low[0], q_high[1], preferred_element_type=F32)
        m_high[...], m_low[...] = split_high_low(product)

    def stage(number):
        @pl.when(group == number)
        def _():
            if number > 0:
                f_copy.wait_recv()
            if number < groups - 1:
                f_out[...] = carry(f_in[...], m_high, m_low, 0)
                f_copy.start()

        @pl.when(group == groups - 1 - number)
        def _():
            if number > 0:
                g_copy.wait_recv()
            if number < groups - 1:
                g_out[...] = carry(g_in[...], m_high, m_low, 1)
                g_copy.start()

    left, right = order[k], order[k + 1]
    pairs = blocks // 2
    meet = min(MEET, QUARTERS * pairs - 1)
    shape = (domain // 32, 32, 128)
    level = lax.broadcasted_iota(jnp.int32, shape, 0) * 32
    level += lax.broadcasted_iota(jnp.int32, shape, 1)
    levels = (level - 128).astype(jnp.int8)

    def multiply(slot):
        acc[...] += lax.dot_general(
            slot[0][...], slot[1][...], (((1,), (1,)), ((), ())),
            preferred_element_type=F32,
        )

    for quarter, tab in enumerate(tabs):
        loads[quarter].wait()

        @pl.loop(0, pairs)
        def _(pair, tab=tab, quarter=quarter):
            for turn in range(2):
                start = (pair * 2 + turn) * BLOCK
                fill_one_hot(tab, left, start, levels, slots[turn][0])
                fill_one_hot(tab, right, start, levels, slots[turn][1])
                multiply(slots[1 - turn])

            @pl.when(quarter * pairs + pair == meet)
            def _():
                pair_product()
                stage(0)

            if groups > 2:

                @pl.when(quarter * pairs + pair == min(meet + 2, QUARTERS * pairs - 1))
                def _():
                    stage(1)

    multiply(slots[1])
    mine, theirs = core * (domain // 2), (1 - core) * (domain // 2)

    def part(base, piece):
        return pl.ds(pl.multiple_of(base + piece * rows, rows), rows)

    first_trip, second_trip, third_trip = [], [], []
    for piece in range(PIECES):
        copy = pltpu.make_async_remote_copy(
            acc.at[part(theirs, piece)], sibling.at[piece],
            send1.at[piece], recv1.at[piece], {"dp": twin}, MESH,
        )
        copy.start()
        first_trip.append(copy)
    for number in range(2, groups - 1):
        stage(number)
    for piece in range(PIECES):
        first_trip[piece].wait_recv()
        half[piece] = acc[part(mine, piece), :] + sibling[piece]
        for step in range(1, chips):
            copy = pltpu.make_async_remote_copy(
                half.at[piece], across.at[step - 1, piece],
                send2.at[step - 1, piece], recv2.at[step - 1, piece],
                {"dp": lax.rem(chip + step, chips) * 2 + core}, MESH,
            )
            copy.start()
            second_trip.append(copy)

    if groups > 1:
        stage(groups - 1)

    @pl.when(odd == 1)
    def _():
        f_own[...] = carry(f_in[...], q_high.at[0], q_low.at[0], 0)
        g_own[...] = g_in[...]

    @pl.when(odd == 0)
    def _():
        f_own[...] = f_in[...]
        g_own[...] = carry(g_in[...], q_high.at[1], q_low.at[1], 1)

    f, g = f_own[...], g_own[...]
    column = jnp.transpose(jnp.broadcast_to(f / jnp.sum(f), (8, domain)))[:, 0:1]
    joint = column * q[odd] * (g / jnp.sum(g))
    beliefs[...] = joint * (float(domain * domain) / jnp.sum(joint))

    put_beliefs = pltpu.make_async_copy(beliefs, beliefs_out, out_sem.at[0])
    put_beliefs.start()

    for piece in range(PIECES):
        summed = half[piece]
        for step in range(1, chips):
            second_trip[piece * (chips - 1) + step - 1].wait_recv()
            summed = summed + across[step - 1, piece]
        total[part(mine, piece), :] = summed
        copy = pltpu.make_async_remote_copy(
            total.at[part(mine, piece)], total.at[part(mine, piece)],
            send3.at[piece], recv3.at[piece], {"dp": twin}, MESH,
        )
        copy.start()
        third_trip.append(copy)

    get_noise.wait()

    def finish(where):
        measured = (total[where, :] + noise[where, :]) * scale
        updated[where, :] = potential[odd, where, :] - step_size * (beliefs[where, :] - measured)

    halves = []
    for number, base in enumerate((mine, theirs)):
        for piece in range(PIECES):
            if number == 1:
                third_trip[piece].wait_recv()
            finish(part(base, piece))
        where = pl.ds(pl.multiple_of(base, domain // 2), domain // 2)
        put = pltpu.make_async_copy(
            updated.at[where], updated_out.at[where], out_sem.at[1 + number]
        )
        put.start()
        halves.append(put)

    for copy in first_trip + second_trip + third_trip:
        copy.wait_send()

    pair_copy.wait_send()
    for copy in [put_beliefs] + halves:
        copy.wait()

    @pl.when(group < groups - 1)
    def _():
        f_copy.wait_send()

    @pl.when(group > 0)
    def _():
        g_copy.wait_send()


def hand_on(updated, beliefs, updated_out, beliefs_out, sems):
    copies = []
    for number, (source, target) in enumerate(((updated, updated_out), (beliefs, beliefs_out))):
        rows = source.shape[0] // 2
        for half in range(2):
            where = pl.ds(half * rows, rows)
            copy = pltpu.make_async_copy(source.at[where], target.at[where], sems.at[number, half])
            copy.start()
            copies.append(copy)
    for copy in copies:
        copy.wait()


def per_device(table_rows, attribute_order, log_potential, measure_noise):
    cliques, copies = lax.axis_size("clique"), lax.axis_size("dp")
    domain = log_potential.shape[1]
    attributes, columns = table_rows.shape
    scale = domain * domain / (columns * copies)
    rows = domain // 2 // PIECES
    chips = copies // 2
    table = jax.ShapeDtypeStruct((domain, domain), F32)
    hbm = pl.BlockSpec(memory_space=pl.ANY)
    dma = pltpu.SemaphoreType.DMA
    updated, beliefs = pl.pallas_call(
        functools.partial(kernel, (cliques, copies), scale),
        out_shape=(table, table),
        in_specs=[
            pl.BlockSpec(memory_space=pltpu.SMEM),
            hbm,
            hbm,
            hbm,
        ],
        out_specs=(hbm, hbm),
        scratch_shapes=[
            [pltpu.VMEM((attributes, columns // QUARTERS), jnp.int32)] * QUARTERS,
            [[pltpu.VMEM((domain, BLOCK), ONE)] * 2] * 2,
            pltpu.VMEM((2, domain, domain), F32),
            pltpu.VMEM((domain, domain), F32),
            pltpu.VMEM((domain, domain), F32),
            pltpu.VMEM((domain, domain), F32),
            pltpu.VMEM((domain, domain), F32),
            pltpu.VMEM((2, domain, domain), F32),
            pltpu.VMEM((2, domain, domain), BF16),
            pltpu.VMEM((2, domain, domain), BF16),
            pltpu.VMEM((domain, domain), BF16),
            pltpu.VMEM((domain, domain), BF16),
            [pltpu.VMEM((1, domain), F32)] * 6,
            pltpu.VMEM((PIECES, rows, domain), F32),
            pltpu.VMEM((PIECES, rows, domain), F32),
            pltpu.VMEM((chips - 1, PIECES, rows, domain), F32),
            pltpu.VMEM((domain, domain), F32),
            dma((QUARTERS,)),
            dma((2,)),
            dma((3,)),
            dma((2,)),
            dma((2,)),
            dma((2,)),
            dma((PIECES,)),
            dma((PIECES,)),
            dma((chips - 1, PIECES)),
            dma((chips - 1, PIECES)),
            dma((PIECES,)),
            dma((PIECES,)),
        ],
        compiler_params=pltpu.CompilerParams(
            collective_id=0, has_side_effects=True, vmem_limit_bytes=VMEM_LIMIT
        ),
    )(attribute_order, table_rows, log_potential, measure_noise)
    updated, beliefs = pl.pallas_call(
        hand_on,
        out_shape=(table, table),
        in_specs=[hbm, hbm],
        out_specs=(hbm, hbm),
        scratch_shapes=[dma((2, 2))],
        compiler_params=pltpu.CompilerParams(vmem_limit_bytes=VMEM_LIMIT),
    )(updated, beliefs)
    return updated[None], beliefs[None]


def solution(mesh):
    in_specs = (P(None, "dp"), P(), P("clique", None, None), P("clique", None, None))
    out_specs = (P("clique", None, None), P("clique", None, None))
    return jax.shard_map(
        per_device, mesh=mesh, in_specs=in_specs, out_specs=out_specs, check_vma=False
    )
```

```python
import functools
import math

import jax
import jax.numpy as jnp
from jax import lax
from jax.experimental import pallas as pl
from jax.experimental.pallas import tpu as pltpu
from jax.sharding import PartitionSpec as P

step_size = 0.25
PIECES = 4
BLOCK = 4096
QUARTERS = 4
MEET = 4
VMEM_LIMIT = 60 * 1024 * 1024
MESH = pl.DeviceIdType.MESH
BF16 = jnp.bfloat16
F32 = jnp.float32
ONE = jnp.float8_e4m3fn


def split_high_low(value):
    high = value.astype(BF16)
    return high, (value - high.astype(F32)).astype(BF16)


def message_rows(vector):
    wide = jnp.broadcast_to(vector, (16, vector.shape[1]))
    high = wide.astype(BF16).astype(F32)
    row = lax.broadcasted_iota(jnp.int32, wide.shape, 0)
    return jnp.where(row < 8, high, wide - high).astype(BF16)


def carry(vector, kernel_high, kernel_low, contract):
    rows = message_rows(vector)
    dims = (((1,), (contract,)), ((), ()))
    moved = lax.dot_general(rows, kernel_high[...], dims, preferred_element_type=F32)
    moved += lax.dot_general(rows, kernel_low[...], dims, preferred_element_type=F32)
    return (moved[0:1] + moved[8:9]) / jnp.sum(vector)


def fill_one_hot(tab, attribute, start, levels, slot):
    kinds, deep, lanes = levels.shape
    width = slot.shape[1]
    values = tab[pl.ds(attribute, 1), pl.ds(pl.multiple_of(start, width), width)] - 128
    for tile in range(0, width, lanes):
        wide = jnp.broadcast_to(values[:, tile : tile + lanes], (deep, lanes))
        hit = wide.astype(jnp.int8)[None] == levels
        ones = jnp.where(hit, jnp.ones((), ONE), jnp.zeros((), ONE))
        slot[:, tile : tile + lanes] = ones.reshape(kinds * deep, lanes)


def kernel(
    sizes, scale, order, table, potential_in, noise_in, updated_out, beliefs_out,
    tabs, slots, potential, noise, updated, beliefs, acc, q, q_high, q_low, m_high, m_low,
    vectors, sibling, half, across, total,
    tab_sem, in_sem, out_sem, pair_sem, f_sem, g_sem, send1, recv1, send2, recv2, send3, recv3,
):
    cliques, copies = sizes
    f_in, f_out, g_in, g_out, f_own, g_own = vectors
    domain = acc.shape[0]
    groups = cliques // 2
    columns = tabs[0].shape[1]
    blocks = columns // BLOCK
    chips = copies // 2
    rows = domain // 2 // PIECES
    k = lax.axis_index("clique")
    d = lax.axis_index("dp")
    chip, core = d // 2, lax.rem(d, 2)
    twin = chip * 2 + 1 - core
    group, odd = k // 2, lax.rem(k, 2)
    partner = group * 2 + 1 - odd

    get_potential = pltpu.make_async_copy(
        potential_in.at[0], potential.at[odd], in_sem.at[0]
    )
    get_potential.start()
    loads = []
    for quarter, tab in enumerate(tabs):
        where = pl.ds(quarter * columns, columns)
        load = pltpu.make_async_copy(table.at[:, where], tab, tab_sem.at[quarter])
        load.start()
        loads.append(load)
    get_noise = pltpu.make_async_copy(noise_in.at[0], noise, in_sem.at[1])
    get_noise.start()

    barrier = pltpu.get_barrier_semaphore()

    def greet(device):
        pl.semaphore_signal(barrier, inc=1, device_id=device, device_id_type=MESH)

    greet({"dp": twin})
    for step in range(1, chips):
        greet({"dp": lax.rem(chip + step, chips) * 2 + core})

    greet({"clique": partner})

    @pl.when(group > 0)
    def _():
        greet({"clique": k - 2})

    @pl.when(group < groups - 1)
    def _():
        greet({"clique": k + 2})

    acc[...] = jnp.zeros_like(acc)
    slots[1][0][...] = jnp.zeros_like(slots[1][0])
    slots[1][1][...] = jnp.zeros_like(slots[1][1])

    @pl.when(group == 0)
    def _():
        f_in[...] = jnp.ones_like(f_in)

    @pl.when(group == groups - 1)
    def _():
        g_in[...] = jnp.ones_like(g_in)

    at_end = jnp.logical_or(group == 0, group == groups - 1)

    @pl.when(at_end)
    def _():
        pl.semaphore_wait(barrier, chips + 2)

    @pl.when(jnp.logical_not(at_end))
    def _():
        pl.semaphore_wait(barrier, chips + 3)

    pair_copy = pltpu.make_async_remote_copy(
        potential_in.at[0], potential.at[odd], pair_sem.at[0], pair_sem.at[1],
        {"clique": partner}, MESH,
    )
    pair_copy.start()
    f_copy = pltpu.make_async_remote_copy(
        f_out, f_in, f_sem.at[0], f_sem.at[1], {"clique": lax.rem(k + 2, cliques)}, MESH
    )
    g_copy = pltpu.make_async_remote_copy(
        g_out, g_in, g_sem.at[0], g_sem.at[1],
        {"clique": lax.rem(k + cliques - 2, cliques)}, MESH,
    )

    def prepare(which):
        q[which] = jnp.exp(potential[which])
        q_high[which], q_low[which] = split_high_low(q[which])

    get_potential.wait()
    prepare(odd)

    def pair_product():
        pair_copy.wait_recv()
        prepare(1 - odd)
        product = jnp.dot(q_high[0], q_high[1], preferred_element_type=F32)
        product += jnp.dot(q_high[0], q_low[1], preferred_element_type=F32)
        product += jnp.dot(q_low[0], q_high[1], preferred_element_type=F32)
        m_high[...], m_low[...] = split_high_low(product)

    def stage(number):
        @pl.when(group == number)
        def _():
            if number > 0:
                f_copy.wait_recv()
            if number < groups - 1:
                f_out[...] = carry(f_in[...], m_high, m_low, 0)
                f_copy.start()

        @pl.when(group == groups - 1 - number)
        def _():
            if number > 0:
                g_copy.wait_recv()
            if number < groups - 1:
                g_out[...] = carry(g_in[...], m_high, m_low, 1)
                g_copy.start()

    left, right = order[k], order[k + 1]
    pairs = blocks // 2
    meet = min(MEET, QUARTERS * pairs - 1)
    shape = (domain // 32, 32, 128)
    level = lax.broadcasted_iota(jnp.int32, shape, 0) * 32
    level += lax.broadcasted_iota(jnp.int32, shape, 1)
    levels = (level - 128).astype(jnp.int8)

    def multiply(slot):
        acc[...] += lax.dot_general(
            slot[0][...], slot[1][...], (((1,), (1,)), ((), ())),
            preferred_element_type=F32,
        )

    for quarter, tab in enumerate(tabs):
        loads[quarter].wait()

        @pl.loop(0, pairs)
        def _(pair, tab=tab, quarter=quarter):
            for turn in range(2):
                multiply(slots[1 - turn])
                start = (pair * 2 + turn) * BLOCK
                fill_one_hot(tab, left, start, levels, slots[turn][0])
                fill_one_hot(tab, right, start, levels, slots[turn][1])

            @pl.when(quarter * pairs + pair == meet)
            def _():
                pair_product()
                stage(0)

            if groups > 2:

                @pl.when(quarter * pairs + pair == min(meet + 2, QUARTERS * pairs - 1))
                def _():
                    stage(1)

    multiply(slots[1])
    mine, theirs = core * (domain // 2), (1 - core) * (domain // 2)

    def part(base, piece):
        return pl.ds(pl.multiple_of(base + piece * rows, rows), rows)

    first_trip, second_trip, third_trip = [], [], []
    for piece in range(PIECES):
        copy = pltpu.make_async_remote_copy(
            acc.at[part(theirs, piece)], sibling.at[piece],
            send1.at[piece], recv1.at[piece], {"dp": twin}, MESH,
        )
        copy.start()
        first_trip.append(copy)
    for number in range(2, groups - 1):
        stage(number)
    for piece in range(PIECES):
        first_trip[piece].wait_recv()
        half[piece] = acc[part(mine, piece), :] + sibling[piece]
        for step in range(1, chips):
            copy = pltpu.make_async_remote_copy(
                half.at[piece], across.at[step - 1, piece],
                send2.at[step - 1, piece], recv2.at[step - 1, piece],
                {"dp": lax.rem(chip + step, chips) * 2 + core}, MESH,
            )
            copy.start()
            second_trip.append(copy)

    if groups > 1:
        stage(groups - 1)

    @pl.when(odd == 1)
    def _():
        f_own[...] = carry(f_in[...], q_high.at[0], q_low.at[0], 0)
        g_own[...] = g_in[...]

    @pl.when(odd == 0)
    def _():
        f_own[...] = f_in[...]
        g_own[...] = carry(g_in[...], q_high.at[1], q_low.at[1], 1)

    f, g = f_own[...], g_own[...]
    column = jnp.transpose(jnp.broadcast_to(f / jnp.sum(f), (8, domain)))[:, 0:1]
    joint = column * q[odd] * (g / jnp.sum(g))
    beliefs[...] = joint * (float(domain * domain) / jnp.sum(joint))

    put_beliefs = pltpu.make_async_copy(beliefs, beliefs_out, out_sem.at[0])
    put_beliefs.start()

    for piece in range(PIECES):
        summed = half[piece]
        for step in range(1, chips):
            second_trip[piece * (chips - 1) + step - 1].wait_recv()
            summed = summed + across[step - 1, piece]
        total[part(mine, piece), :] = summed
        copy = pltpu.make_async_remote_copy(
            total.at[part(mine, piece)], total.at[part(mine, piece)],
            send3.at[piece], recv3.at[piece], {"dp": twin}, MESH,
        )
        copy.start()
        third_trip.append(copy)

    get_noise.wait()

    def finish(where):
        measured = (total[where, :] + noise[where, :]) * scale
        updated[where, :] = potential[odd, where, :] - step_size * (beliefs[where, :] - measured)

    halves = []
    for number, base in enumerate((mine, theirs)):
        for piece in range(PIECES):
            if number == 1:
                third_trip[piece].wait_recv()
            finish(part(base, piece))
        where = pl.ds(pl.multiple_of(base, domain // 2), domain // 2)
        put = pltpu.make_async_copy(
            updated.at[where], updated_out.at[where], out_sem.at[1 + number]
        )
        put.start()
        halves.append(put)

    for copy in first_trip + second_trip + third_trip:
        copy.wait_send()

    pair_copy.wait_send()
    for copy in [put_beliefs] + halves:
        copy.wait()

    @pl.when(group < groups - 1)
    def _():
        f_copy.wait_send()

    @pl.when(group > 0)
    def _():
        g_copy.wait_send()


def hand_on(updated, beliefs, updated_out, beliefs_out, held, get_sem, put_sem):
    rows = updated.shape[0] // 2
    parts = []
    for number, (source, target) in enumerate(((updated, updated_out), (beliefs, beliefs_out))):
        for half in range(2):
            where, slot = pl.ds(half * rows, rows), held.at[number, half]
            get = pltpu.make_async_copy(source.at[where], slot, get_sem.at[number, half])
            put = pltpu.make_async_copy(slot, target.at[where], put_sem.at[number, half])
            get.start()
            parts.append((get, put))
    for get, put in parts:
        get.wait()
        put.start()
    for get, put in parts:
        put.wait()


def per_device(table_rows, attribute_order, log_potential, measure_noise):
    cliques, copies = lax.axis_size("clique"), lax.axis_size("dp")
    domain = log_potential.shape[1]
    attributes, columns = table_rows.shape
    scale = domain * domain / (columns * copies)
    rows = domain // 2 // PIECES
    chips = copies // 2
    table = jax.ShapeDtypeStruct((domain, domain), F32)
    hbm = pl.BlockSpec(memory_space=pl.ANY)
    dma = pltpu.SemaphoreType.DMA
    updated, beliefs = pl.pallas_call(
        functools.partial(kernel, (cliques, copies), scale),
        out_shape=(table, table),
        in_specs=[
            pl.BlockSpec(memory_space=pltpu.SMEM),
            hbm,
            hbm,
            hbm,
        ],
        out_specs=(hbm, hbm),
        scratch_shapes=[
            [pltpu.VMEM((attributes, columns // QUARTERS), jnp.int32)] * QUARTERS,
            [[pltpu.VMEM((domain, BLOCK), ONE)] * 2] * 2,
            pltpu.VMEM((2, domain, domain), F32),
            pltpu.VMEM((domain, domain), F32),
            pltpu.VMEM((domain, domain), F32),
            pltpu.VMEM((domain, domain), F32),
            pltpu.VMEM((domain, domain), F32),
            pltpu.VMEM((2, domain, domain), F32),
            pltpu.VMEM((2, domain, domain), BF16),
            pltpu.VMEM((2, domain, domain), BF16),
            pltpu.VMEM((domain, domain), BF16),
            pltpu.VMEM((domain, domain), BF16),
            [pltpu.VMEM((1, domain), F32)] * 6,
            pltpu.VMEM((PIECES, rows, domain), F32),
            pltpu.VMEM((PIECES, rows, domain), F32),
            pltpu.VMEM((chips - 1, PIECES, rows, domain), F32),
            pltpu.VMEM((domain, domain), F32),
            dma((QUARTERS,)),
            dma((2,)),
            dma((3,)),
            dma((2,)),
            dma((2,)),
            dma((2,)),
            dma((PIECES,)),
            dma((PIECES,)),
            dma((chips - 1, PIECES)),
            dma((chips - 1, PIECES)),
            dma((PIECES,)),
            dma((PIECES,)),
        ],
        compiler_params=pltpu.CompilerParams(
            collective_id=0, has_side_effects=True, vmem_limit_bytes=VMEM_LIMIT
        ),
    )(attribute_order, table_rows, log_potential, measure_noise)
    updated, beliefs = pl.pallas_call(
        hand_on,
        out_shape=(table, table),
        in_specs=[hbm, hbm],
        out_specs=(hbm, hbm),
        scratch_shapes=[
            pltpu.VMEM((2, 2, domain // 2, domain), F32), dma((2, 2)), dma((2, 2)),
        ],
        compiler_params=pltpu.CompilerParams(vmem_limit_bytes=VMEM_LIMIT),
    )(updated, beliefs)
    return updated[None], beliefs[None]


def solution(mesh):
    in_specs = (P(None, "dp"), P(), P("clique", None, None), P("clique", None, None))
    out_specs = (P("clique", None, None), P("clique", None, None))
    return jax.shard_map(
        per_device, mesh=mesh, in_specs=in_specs, out_specs=out_specs, check_vma=False
    )
```

```python
import functools
import math

import jax
import jax.numpy as jnp
from jax import lax
from jax.experimental import pallas as pl
from jax.experimental.pallas import tpu as pltpu
from jax.sharding import PartitionSpec as P

step_size = 0.25
PIECES = 4
BLOCK = 4096
QUARTERS = 4
MEET = 4
VMEM_LIMIT = 60 * 1024 * 1024
MESH = pl.DeviceIdType.MESH
BF16 = jnp.bfloat16
F32 = jnp.float32
ONE = jnp.float8_e4m3fn


def split_high_low(value):
    high = value.astype(BF16)
    return high, (value - high.astype(F32)).astype(BF16)


def message_rows(vector):
    wide = jnp.broadcast_to(vector, (16, vector.shape[1]))
    high = wide.astype(BF16).astype(F32)
    row = lax.broadcasted_iota(jnp.int32, wide.shape, 0)
    return jnp.where(row < 8, high, wide - high).astype(BF16)


def carry(vector, kernel_high, kernel_low, contract):
    rows = message_rows(vector)
    dims = (((1,), (contract,)), ((), ()))
    moved = lax.dot_general(rows, kernel_high[...], dims, preferred_element_type=F32)
    moved += lax.dot_general(rows, kernel_low[...], dims, preferred_element_type=F32)
    return (moved[0:1] + moved[8:9]) / jnp.sum(vector)


def fill_one_hot(tab, attribute, start, levels, slot):
    kinds, deep, lanes = levels.shape
    width = slot.shape[1]
    values = tab[pl.ds(attribute, 1), pl.ds(pl.multiple_of(start, width), width)] - 128
    for tile in range(0, width, lanes):
        wide = jnp.broadcast_to(values[:, tile : tile + lanes], (deep, lanes))
        hit = wide.astype(jnp.int8)[None] == levels
        ones = jnp.where(hit, jnp.ones((), ONE), jnp.zeros((), ONE))
        slot[:, tile : tile + lanes] = ones.reshape(kinds * deep, lanes)


def kernel(
    sizes, scale, order, table, potential_in, noise_in, updated_out, beliefs_out,
    tabs, slots, potential, noise, updated, beliefs, acc, q, q_high, q_low, m_high, m_low,
    vectors, sibling, half, across, total,
    tab_sem, in_sem, out_sem, pair_sem, f_sem, g_sem, send1, recv1, send2, recv2, send3, recv3,
):
    cliques, copies = sizes
    f_in, f_out, g_in, g_out, f_own, g_own = vectors
    domain = acc.shape[0]
    groups = cliques // 2
    columns = tabs[0].shape[1]
    blocks = columns // BLOCK
    chips = copies // 2
    rows = domain // 2 // PIECES
    k = lax.axis_index("clique")
    d = lax.axis_index("dp")
    chip, core = d // 2, lax.rem(d, 2)
    twin = chip * 2 + 1 - core
    group, odd = k // 2, lax.rem(k, 2)
    partner = group * 2 + 1 - odd

    get_potential = pltpu.make_async_copy(
        potential_in.at[0], potential.at[odd], in_sem.at[0]
    )
    get_potential.start()
    loads = []
    for quarter, tab in enumerate(tabs):
        where = pl.ds(quarter * columns, columns)
        load = pltpu.make_async_copy(table.at[:, where], tab, tab_sem.at[quarter])
        load.start()
        loads.append(load)
    get_noise = pltpu.make_async_copy(noise_in.at[0], noise, in_sem.at[1])
    get_noise.start()

    barrier = pltpu.get_barrier_semaphore()

    def greet(device):
        pl.semaphore_signal(barrier, inc=1, device_id=device, device_id_type=MESH)

    greet({"dp": twin})
    for step in range(1, chips):
        greet({"dp": lax.rem(chip + step, chips) * 2 + core})

    greet({"clique": partner})

    @pl.when(group > 0)
    def _():
        greet({"clique": k - 2})

    @pl.when(group < groups - 1)
    def _():
        greet({"clique": k + 2})

    acc[...] = jnp.zeros_like(acc)
    slots[1][0][...] = jnp.zeros_like(slots[1][0])
    slots[1][1][...] = jnp.zeros_like(slots[1][1])

    @pl.when(k == 0)
    def _():
        f_in[...] = jnp.ones_like(f_in)

    @pl.when(k == cliques - 1)
    def _():
        g_in[...] = jnp.ones_like(g_in)

    second, before_last = k == 1, k == cliques - 2

    @pl.when(jnp.logical_or(second, k == cliques - 3))
    def _():
        greet({"clique": k + 1})

    @pl.when(jnp.logical_or(k == 2, before_last))
    def _():
        greet({"clique": k - 1})

    inner = jnp.logical_and(group > 0, group < groups - 1)
    crossing = (k == 1, k == 2, k == cliques - 3, k == cliques - 2)
    extra = sum(jnp.where(one, 1, 0) for one in crossing)
    pl.semaphore_wait(barrier, chips + 2 + jnp.where(inner, 1, 0) + extra)

    pair_copy = pltpu.make_async_remote_copy(
        potential_in.at[0], potential.at[odd], pair_sem.at[0], pair_sem.at[1],
        {"clique": partner}, MESH,
    )
    pair_copy.start()
    f_copy = pltpu.make_async_remote_copy(
        f_out, f_in, f_sem.at[0], f_sem.at[1],
        {"clique": jnp.where(k == 0, 1, lax.rem(k + 2, cliques))}, MESH,
    )
    f_cross = pltpu.make_async_remote_copy(
        f_out, f_in, f_sem.at[2], f_sem.at[1], {"clique": lax.rem(k + 1, cliques)}, MESH
    )
    g_copy = pltpu.make_async_remote_copy(
        g_out, g_in, g_sem.at[0], g_sem.at[1],
        {"clique": jnp.where(k == cliques - 1, k - 1, lax.rem(k + cliques - 2, cliques))},
        MESH,
    )
    g_cross = pltpu.make_async_remote_copy(
        g_out, g_in, g_sem.at[2], g_sem.at[1],
        {"clique": lax.rem(k + cliques - 1, cliques)}, MESH,
    )

    def prepare(which):
        q[which] = jnp.exp(potential[which])
        q_high[which], q_low[which] = split_high_low(q[which])

    get_potential.wait()
    prepare(odd)

    @pl.when(k == 0)
    def _():
        f_out[...] = carry(f_in[...], q_high.at[0], q_low.at[0], 0)
        f_copy.start()

    @pl.when(k == cliques - 1)
    def _():
        g_out[...] = carry(g_in[...], q_high.at[1], q_low.at[1], 1)
        g_copy.start()

    def second_messages():
        @pl.when(second)
        def _():
            f_copy.wait_recv()
            f_out[...] = carry(f_in[...], q_high.at[1], q_low.at[1], 0)
            f_copy.start()
            f_cross.start()

        @pl.when(before_last)
        def _():
            g_copy.wait_recv()
            g_out[...] = carry(g_in[...], q_high.at[0], q_low.at[0], 1)
            g_copy.start()
            g_cross.start()

    def pair_product():
        pair_copy.wait_recv()
        prepare(1 - odd)

        @pl.when(inner)
        def _():
            product = jnp.dot(q_high[0], q_high[1], preferred_element_type=F32)
            product += jnp.dot(q_high[0], q_low[1], preferred_element_type=F32)
            product += jnp.dot(q_low[0], q_high[1], preferred_element_type=F32)
            m_high[...], m_low[...] = split_high_low(product)

    def stage(number):
        @pl.when(group == number)
        def _():
            f_copy.wait_recv()
            if number < groups - 1:
                f_out[...] = carry(f_in[...], m_high, m_low, 0)
                f_copy.start()

        @pl.when(group == groups - 1 - number)
        def _():
            g_copy.wait_recv()
            if number < groups - 1:
                g_out[...] = carry(g_in[...], m_high, m_low, 1)
                g_copy.start()

    left, right = order[k], order[k + 1]
    pairs = blocks // 2
    meet = min(MEET, QUARTERS * pairs - 1)
    shape = (domain // 32, 32, 128)
    level = lax.broadcasted_iota(jnp.int32, shape, 0) * 32
    level += lax.broadcasted_iota(jnp.int32, shape, 1)
    levels = (level - 128).astype(jnp.int8)

    def multiply(slot):
        acc[...] += lax.dot_general(
            slot[0][...], slot[1][...], (((1,), (1,)), ((), ())),
            preferred_element_type=F32,
        )

    for quarter, tab in enumerate(tabs):
        loads[quarter].wait()

        @pl.loop(0, pairs)
        def _(pair, tab=tab, quarter=quarter):
            for turn in range(2):
                multiply(slots[1 - turn])
                start = (pair * 2 + turn) * BLOCK
                fill_one_hot(tab, left, start, levels, slots[turn][0])
                fill_one_hot(tab, right, start, levels, slots[turn][1])

            done = quarter * pairs + pair
            pl.when(done == 1)(second_messages)

            @pl.when(done == meet)
            def _():
                pair_product()
                stage(1)

    multiply(slots[1])
    mine, theirs = core * (domain // 2), (1 - core) * (domain // 2)

    def part(base, piece):
        return pl.ds(pl.multiple_of(base + piece * rows, rows), rows)

    first_trip, second_trip, third_trip = [], [], []
    for piece in range(PIECES):
        copy = pltpu.make_async_remote_copy(
            acc.at[part(theirs, piece)], sibling.at[piece],
            send1.at[piece], recv1.at[piece], {"dp": twin}, MESH,
        )
        copy.start()
        first_trip.append(copy)
    for number in range(2, groups - 1):
        stage(number)
    for piece in range(PIECES):
        first_trip[piece].wait_recv()
        half[piece] = acc[part(mine, piece), :] + sibling[piece]
        for step in range(1, chips):
            copy = pltpu.make_async_remote_copy(
                half.at[piece], across.at[step - 1, piece],
                send2.at[step - 1, piece], recv2.at[step - 1, piece],
                {"dp": lax.rem(chip + step, chips) * 2 + core}, MESH,
            )
            copy.start()
            second_trip.append(copy)

    stage(groups - 1)

    f_own[...] = f_in[...]
    g_own[...] = g_in[...]

    @pl.when(jnp.logical_and(odd == 1, k > 1))
    def _():
        f_own[...] = carry(f_in[...], q_high.at[0], q_low.at[0], 0)

    @pl.when(jnp.logical_and(odd == 0, k < cliques - 2))
    def _():
        g_own[...] = carry(g_in[...], q_high.at[1], q_low.at[1], 1)

    f, g = f_own[...], g_own[...]
    column = jnp.transpose(jnp.broadcast_to(f / jnp.sum(f), (8, domain)))[:, 0:1]
    joint = column * q[odd] * (g / jnp.sum(g))
    beliefs[...] = joint * (float(domain * domain) / jnp.sum(joint))

    put_beliefs = pltpu.make_async_copy(beliefs, beliefs_out, out_sem.at[0])
    put_beliefs.start()

    for piece in range(PIECES):
        summed = half[piece]
        for step in range(1, chips):
            second_trip[piece * (chips - 1) + step - 1].wait_recv()
            summed = summed + across[step - 1, piece]
        total[part(mine, piece), :] = summed
        copy = pltpu.make_async_remote_copy(
            total.at[part(mine, piece)], total.at[part(mine, piece)],
            send3.at[piece], recv3.at[piece], {"dp": twin}, MESH,
        )
        copy.start()
        third_trip.append(copy)

    get_noise.wait()

    def finish(where):
        measured = (total[where, :] + noise[where, :]) * scale
        updated[where, :] = potential[odd, where, :] - step_size * (beliefs[where, :] - measured)

    halves = []
    for number, base in enumerate((mine, theirs)):
        for piece in range(PIECES):
            if number == 1:
                third_trip[piece].wait_recv()
            finish(part(base, piece))
        where = pl.ds(pl.multiple_of(base, domain // 2), domain // 2)
        put = pltpu.make_async_copy(
            updated.at[where], updated_out.at[where], out_sem.at[1 + number]
        )
        put.start()
        halves.append(put)

    for copy in first_trip + second_trip + third_trip:
        copy.wait_send()

    pair_copy.wait_send()
    for copy in [put_beliefs] + halves:
        copy.wait()

    @pl.when(group < groups - 1)
    def _():
        f_copy.wait_send()

    @pl.when(group > 0)
    def _():
        g_copy.wait_send()

    @pl.when(second)
    def _():
        f_cross.wait_send()

    @pl.when(before_last)
    def _():
        g_cross.wait_send()


def hand_on(updated, beliefs, updated_out, beliefs_out, held, get_sem, put_sem):
    rows = updated.shape[0] // 2
    parts = []
    for number, (source, target) in enumerate(((updated, updated_out), (beliefs, beliefs_out))):
        for half in range(2):
            where, slot = pl.ds(half * rows, rows), held.at[number, half]
            get = pltpu.make_async_copy(source.at[where], slot, get_sem.at[number, half])
            put = pltpu.make_async_copy(slot, target.at[where], put_sem.at[number, half])
            get.start()
            parts.append((get, put))
    for get, put in parts:
        get.wait()
        put.start()
    for get, put in parts:
        put.wait()


def per_device(table_rows, attribute_order, log_potential, measure_noise):
    cliques, copies = lax.axis_size("clique"), lax.axis_size("dp")
    domain = log_potential.shape[1]
    attributes, columns = table_rows.shape
    scale = domain * domain / (columns * copies)
    rows = domain // 2 // PIECES
    chips = copies // 2
    table = jax.ShapeDtypeStruct((domain, domain), F32)
    hbm = pl.BlockSpec(memory_space=pl.ANY)
    dma = pltpu.SemaphoreType.DMA
    updated, beliefs = pl.pallas_call(
        functools.partial(kernel, (cliques, copies), scale),
        out_shape=(table, table),
        in_specs=[
            pl.BlockSpec(memory_space=pltpu.SMEM),
            hbm,
            hbm,
            hbm,
        ],
        out_specs=(hbm, hbm),
        scratch_shapes=[
            [pltpu.VMEM((attributes, columns // QUARTERS), jnp.int32)] * QUARTERS,
            [[pltpu.VMEM((domain, BLOCK), ONE)] * 2] * 2,
            pltpu.VMEM((2, domain, domain), F32),
            pltpu.VMEM((domain, domain), F32),
            pltpu.VMEM((domain, domain), F32),
            pltpu.VMEM((domain, domain), F32),
            pltpu.VMEM((domain, domain), F32),
            pltpu.VMEM((2, domain, domain), F32),
            pltpu.VMEM((2, domain, domain), BF16),
            pltpu.VMEM((2, domain, domain), BF16),
            pltpu.VMEM((domain, domain), BF16),
            pltpu.VMEM((domain, domain), BF16),
            [pltpu.VMEM((1, domain), F32)] * 6,
            pltpu.VMEM((PIECES, rows, domain), F32),
            pltpu.VMEM((PIECES, rows, domain), F32),
            pltpu.VMEM((chips - 1, PIECES, rows, domain), F32),
            pltpu.VMEM((domain, domain), F32),
            dma((QUARTERS,)),
            dma((2,)),
            dma((3,)),
            dma((2,)),
            dma((3,)),
            dma((3,)),
            dma((PIECES,)),
            dma((PIECES,)),
            dma((chips - 1, PIECES)),
            dma((chips - 1, PIECES)),
            dma((PIECES,)),
            dma((PIECES,)),
        ],
        compiler_params=pltpu.CompilerParams(
            collective_id=0, has_side_effects=True, vmem_limit_bytes=VMEM_LIMIT
        ),
    )(attribute_order, table_rows, log_potential, measure_noise)
    updated, beliefs = pl.pallas_call(
        hand_on,
        out_shape=(table, table),
        in_specs=[hbm, hbm],
        out_specs=(hbm, hbm),
        scratch_shapes=[
            pltpu.VMEM((2, 2, domain // 2, domain), F32), dma((2, 2)), dma((2, 2)),
        ],
        compiler_params=pltpu.CompilerParams(vmem_limit_bytes=VMEM_LIMIT),
    )(updated, beliefs)
    return updated[None], beliefs[None]


def solution(mesh):
    in_specs = (P(None, "dp"), P(), P("clique", None, None), P("clique", None, None))
    out_specs = (P("clique", None, None), P("clique", None, None))
    return jax.shard_map(
        per_device, mesh=mesh, in_specs=in_specs, out_specs=out_specs, check_vma=False
    )
```

```python
import functools
import math

import jax
import jax.numpy as jnp
from jax import lax
from jax.experimental import pallas as pl
from jax.experimental.pallas import tpu as pltpu
from jax.sharding import PartitionSpec as P

step_size = 0.25
PIECES = 4
BLOCK = 4096
QUARTERS = 4
RELAY = 2
MEET = 5
VMEM_LIMIT = 60 * 1024 * 1024
MESH = pl.DeviceIdType.MESH
BF16 = jnp.bfloat16
F32 = jnp.float32
ONE = jnp.float8_e4m3fn


def split_high_low(value):
    high = value.astype(BF16)
    return high, (value - high.astype(F32)).astype(BF16)


def message_rows(vector):
    wide = jnp.broadcast_to(vector, (16, vector.shape[1]))
    high = wide.astype(BF16).astype(F32)
    row = lax.broadcasted_iota(jnp.int32, wide.shape, 0)
    return jnp.where(row < 8, high, wide - high).astype(BF16)


def carry(vector, kernel_high, kernel_low, contract):
    rows = message_rows(vector)
    dims = (((1,), (contract,)), ((), ()))
    moved = lax.dot_general(rows, kernel_high[...], dims, preferred_element_type=F32)
    moved += lax.dot_general(rows, kernel_low[...], dims, preferred_element_type=F32)
    return (moved[0:1] + moved[8:9]) / jnp.sum(vector)


def fill_one_hot(tab, attribute, start, levels, slot):
    kinds, deep, lanes = levels.shape
    width = slot.shape[1]
    values = tab[pl.ds(attribute, 1), pl.ds(pl.multiple_of(start, width), width)] - 128
    for tile in range(0, width, lanes):
        wide = jnp.broadcast_to(values[:, tile : tile + lanes], (deep, lanes))
        hit = wide.astype(jnp.int8)[None] == levels
        ones = jnp.where(hit, jnp.ones((), ONE), jnp.zeros((), ONE))
        slot[:, tile : tile + lanes] = ones.reshape(kinds * deep, lanes)


def kernel(
    sizes, scale, order, table, potential_in, noise_in, updated_out, beliefs_out,
    tabs, slots, potential, noise, updated, beliefs, acc, q, q_high, q_low, m_high, m_low,
    vectors, sibling, half, across, total,
    tab_sem, in_sem, out_sem, pair_sem, f_sem, g_sem, send1, recv1, send2, recv2, send3, recv3,
):
    cliques, copies = sizes
    f_in, f_out, g_in, g_out, f_own, g_own = vectors
    domain = acc.shape[0]
    groups = cliques // 2
    columns = tabs[0].shape[1]
    blocks = columns // BLOCK
    chips = copies // 2
    rows = domain // 2 // PIECES
    k = lax.axis_index("clique")
    d = lax.axis_index("dp")
    chip, core = d // 2, lax.rem(d, 2)
    twin = chip * 2 + 1 - core
    group, odd = k // 2, lax.rem(k, 2)
    partner = group * 2 + 1 - odd

    get_potential = pltpu.make_async_copy(
        potential_in.at[0], potential.at[odd], in_sem.at[0]
    )
    get_potential.start()
    loads = []
    for quarter, tab in enumerate(tabs):
        where = pl.ds(quarter * columns, columns)
        load = pltpu.make_async_copy(table.at[:, where], tab, tab_sem.at[quarter])
        load.start()
        loads.append(load)
    get_noise = pltpu.make_async_copy(noise_in.at[0], noise, in_sem.at[1])
    get_noise.start()

    barrier = pltpu.get_barrier_semaphore()

    def greet(device):
        pl.semaphore_signal(barrier, inc=1, device_id=device, device_id_type=MESH)

    greet({"dp": twin})
    for step in range(1, chips):
        greet({"dp": lax.rem(chip + step, chips) * 2 + core})

    greet({"clique": partner})

    @pl.when(group > 0)
    def _():
        greet({"clique": k - 2})

    @pl.when(group < groups - 1)
    def _():
        greet({"clique": k + 2})

    acc[...] = jnp.zeros_like(acc)
    slots[1][0][...] = jnp.zeros_like(slots[1][0])
    slots[1][1][...] = jnp.zeros_like(slots[1][1])

    @pl.when(k == 0)
    def _():
        f_in[...] = jnp.ones_like(f_in)

    @pl.when(k == cliques - 1)
    def _():
        g_in[...] = jnp.ones_like(g_in)

    second, before_last = k == 1, k == cliques - 2

    @pl.when(jnp.logical_or(second, k == cliques - 3))
    def _():
        greet({"clique": k + 1})

    @pl.when(jnp.logical_or(k == 2, before_last))
    def _():
        greet({"clique": k - 1})

    inner = jnp.logical_and(group > 0, group < groups - 1)
    crossing = (k == 1, k == 2, k == cliques - 3, k == cliques - 2)
    extra = sum(jnp.where(one, 1, 0) for one in crossing)
    pl.semaphore_wait(barrier, chips + 2 + jnp.where(inner, 1, 0) + extra)

    share = pl.ds(pl.multiple_of(core * (domain // 2), domain // 2), domain // 2)
    pair_copy = pltpu.make_async_remote_copy(
        potential_in.at[0, share], potential.at[odd, share],
        pair_sem.at[0], pair_sem.at[1], {"clique": partner}, MESH,
    )
    relay = pltpu.make_async_remote_copy(
        potential.at[1 - odd, share], potential.at[1 - odd, share],
        pair_sem.at[2], pair_sem.at[3], {"dp": twin}, MESH,
    )
    pair_copy.start()
    f_copy = pltpu.make_async_remote_copy(
        f_out, f_in, f_sem.at[0], f_sem.at[1],
        {"clique": jnp.where(k == 0, 1, lax.rem(k + 2, cliques))}, MESH,
    )
    f_cross = pltpu.make_async_remote_copy(
        f_out, f_in, f_sem.at[2], f_sem.at[1], {"clique": lax.rem(k + 1, cliques)}, MESH
    )
    g_copy = pltpu.make_async_remote_copy(
        g_out, g_in, g_sem.at[0], g_sem.at[1],
        {"clique": jnp.where(k == cliques - 1, k - 1, lax.rem(k + cliques - 2, cliques))},
        MESH,
    )
    g_cross = pltpu.make_async_remote_copy(
        g_out, g_in, g_sem.at[2], g_sem.at[1],
        {"clique": lax.rem(k + cliques - 1, cliques)}, MESH,
    )

    def prepare(which):
        q[which] = jnp.exp(potential[which])
        q_high[which], q_low[which] = split_high_low(q[which])

    get_potential.wait()
    prepare(odd)

    @pl.when(k == 0)
    def _():
        f_out[...] = carry(f_in[...], q_high.at[0], q_low.at[0], 0)
        f_copy.start()

    @pl.when(k == cliques - 1)
    def _():
        g_out[...] = carry(g_in[...], q_high.at[1], q_low.at[1], 1)
        g_copy.start()

    def second_messages():
        @pl.when(second)
        def _():
            f_copy.wait_recv()
            f_out[...] = carry(f_in[...], q_high.at[1], q_low.at[1], 0)
            f_copy.start()
            f_cross.start()

        @pl.when(before_last)
        def _():
            g_copy.wait_recv()
            g_out[...] = carry(g_in[...], q_high.at[0], q_low.at[0], 1)
            g_copy.start()
            g_cross.start()

    def pass_on():
        pair_copy.wait_recv()
        relay.start()

    def take_partner():
        relay.wait_recv()
        prepare(1 - odd)

    def pair_product():
        @pl.when(inner)
        def _():
            take_partner()
            product = jnp.dot(q_high[0], q_high[1], preferred_element_type=F32)
            product += jnp.dot(q_high[0], q_low[1], preferred_element_type=F32)
            product += jnp.dot(q_low[0], q_high[1], preferred_element_type=F32)
            m_high[...], m_low[...] = split_high_low(product)

    def stage(number):
        @pl.when(group == number)
        def _():
            f_copy.wait_recv()
            if number < groups - 1:
                f_out[...] = carry(f_in[...], m_high, m_low, 0)
                f_copy.start()

        @pl.when(group == groups - 1 - number)
        def _():
            g_copy.wait_recv()
            if number < groups - 1:
                g_out[...] = carry(g_in[...], m_high, m_low, 1)
                g_copy.start()

    left, right = order[k], order[k + 1]
    pairs = blocks // 2
    meet = min(MEET, QUARTERS * pairs - 1)
    shape = (domain // 32, 32, 128)
    level = lax.broadcasted_iota(jnp.int32, shape, 0) * 32
    level += lax.broadcasted_iota(jnp.int32, shape, 1)
    levels = (level - 128).astype(jnp.int8)

    def multiply(slot):
        acc[...] += lax.dot_general(
            slot[0][...], slot[1][...], (((1,), (1,)), ((), ())),
            preferred_element_type=F32,
        )

    for quarter, tab in enumerate(tabs):
        loads[quarter].wait()

        @pl.loop(0, pairs)
        def _(pair, tab=tab, quarter=quarter):
            for turn in range(2):
                multiply(slots[1 - turn])
                start = (pair * 2 + turn) * BLOCK
                fill_one_hot(tab, left, start, levels, slots[turn][0])
                fill_one_hot(tab, right, start, levels, slots[turn][1])

            done = quarter * pairs + pair
            pl.when(done == 1)(second_messages)
            pl.when(done == min(RELAY, meet))(pass_on)

            @pl.when(done == meet)
            def _():
                pair_product()
                stage(1)

    multiply(slots[1])
    mine, theirs = core * (domain // 2), (1 - core) * (domain // 2)

    def part(base, piece):
        return pl.ds(pl.multiple_of(base + piece * rows, rows), rows)

    first_trip, second_trip, third_trip = [], [], []
    for piece in range(PIECES):
        copy = pltpu.make_async_remote_copy(
            acc.at[part(theirs, piece)], sibling.at[piece],
            send1.at[piece], recv1.at[piece], {"dp": twin}, MESH,
        )
        copy.start()
        first_trip.append(copy)
    for number in range(2, groups - 1):
        stage(number)
    for piece in range(PIECES):
        first_trip[piece].wait_recv()
        half[piece] = acc[part(mine, piece), :] + sibling[piece]
        for step in range(1, chips):
            copy = pltpu.make_async_remote_copy(
                half.at[piece], across.at[step - 1, piece],
                send2.at[step - 1, piece], recv2.at[step - 1, piece],
                {"dp": lax.rem(chip + step, chips) * 2 + core}, MESH,
            )
            copy.start()
            second_trip.append(copy)

    pl.when(jnp.logical_not(inner))(take_partner)
    stage(groups - 1)

    f_own[...] = f_in[...]
    g_own[...] = g_in[...]

    @pl.when(jnp.logical_and(odd == 1, k > 1))
    def _():
        f_own[...] = carry(f_in[...], q_high.at[0], q_low.at[0], 0)

    @pl.when(jnp.logical_and(odd == 0, k < cliques - 2))
    def _():
        g_own[...] = carry(g_in[...], q_high.at[1], q_low.at[1], 1)

    f, g = f_own[...], g_own[...]
    column = jnp.transpose(jnp.broadcast_to(f / jnp.sum(f), (8, domain)))[:, 0:1]
    joint = column * q[odd] * (g / jnp.sum(g))
    beliefs[...] = joint * (float(domain * domain) / jnp.sum(joint))

    put_beliefs = pltpu.make_async_copy(beliefs, beliefs_out, out_sem.at[0])
    put_beliefs.start()

    for piece in range(PIECES):
        summed = half[piece]
        for step in range(1, chips):
            second_trip[piece * (chips - 1) + step - 1].wait_recv()
            summed = summed + across[step - 1, piece]
        total[part(mine, piece), :] = summed
        copy = pltpu.make_async_remote_copy(
            total.at[part(mine, piece)], total.at[part(mine, piece)],
            send3.at[piece], recv3.at[piece], {"dp": twin}, MESH,
        )
        copy.start()
        third_trip.append(copy)

    get_noise.wait()

    def finish(where):
        measured = (total[where, :] + noise[where, :]) * scale
        updated[where, :] = potential[odd, where, :] - step_size * (beliefs[where, :] - measured)

    halves = []
    for number, base in enumerate((mine, theirs)):
        for piece in range(PIECES):
            if number == 1:
                third_trip[piece].wait_recv()
            finish(part(base, piece))
        where = pl.ds(pl.multiple_of(base, domain // 2), domain // 2)
        put = pltpu.make_async_copy(
            updated.at[where], updated_out.at[where], out_sem.at[1 + number]
        )
        put.start()
        halves.append(put)

    for copy in first_trip + second_trip + third_trip:
        copy.wait_send()

    pair_copy.wait_send()
    relay.wait_send()
    for copy in [put_beliefs] + halves:
        copy.wait()

    @pl.when(group < groups - 1)
    def _():
        f_copy.wait_send()

    @pl.when(group > 0)
    def _():
        g_copy.wait_send()

    @pl.when(second)
    def _():
        f_cross.wait_send()

    @pl.when(before_last)
    def _():
        g_cross.wait_send()


def hand_on(updated, beliefs, updated_out, beliefs_out, held, get_sem, put_sem):
    rows = updated.shape[0] // 2
    parts = []
    for number, (source, target) in enumerate(((updated, updated_out), (beliefs, beliefs_out))):
        for half in range(2):
            where, slot = pl.ds(half * rows, rows), held.at[number, half]
            get = pltpu.make_async_copy(source.at[where], slot, get_sem.at[number, half])
            put = pltpu.make_async_copy(slot, target.at[where], put_sem.at[number, half])
            get.start()
            parts.append((get, put))
    for get, put in parts:
        get.wait()
        put.start()
    for get, put in parts:
        put.wait()


def per_device(table_rows, attribute_order, log_potential, measure_noise):
    cliques, copies = lax.axis_size("clique"), lax.axis_size("dp")
    domain = log_potential.shape[1]
    attributes, columns = table_rows.shape
    scale = domain * domain / (columns * copies)
    rows = domain // 2 // PIECES
    chips = copies // 2
    table = jax.ShapeDtypeStruct((domain, domain), F32)
    hbm = pl.BlockSpec(memory_space=pl.ANY)
    dma = pltpu.SemaphoreType.DMA
    updated, beliefs = pl.pallas_call(
        functools.partial(kernel, (cliques, copies), scale),
        out_shape=(table, table),
        in_specs=[
            pl.BlockSpec(memory_space=pltpu.SMEM),
            hbm,
            hbm,
            hbm,
        ],
        out_specs=(hbm, hbm),
        scratch_shapes=[
            [pltpu.VMEM((attributes, columns // QUARTERS), jnp.int32)] * QUARTERS,
            [[pltpu.VMEM((domain, BLOCK), ONE)] * 2] * 2,
            pltpu.VMEM((2, domain, domain), F32),
            pltpu.VMEM((domain, domain), F32),
            pltpu.VMEM((domain, domain), F32),
            pltpu.VMEM((domain, domain), F32),
            pltpu.VMEM((domain, domain), F32),
            pltpu.VMEM((2, domain, domain), F32),
            pltpu.VMEM((2, domain, domain), BF16),
            pltpu.VMEM((2, domain, domain), BF16),
            pltpu.VMEM((domain, domain), BF16),
            pltpu.VMEM((domain, domain), BF16),
            [pltpu.VMEM((1, domain), F32)] * 6,
            pltpu.VMEM((PIECES, rows, domain), F32),
            pltpu.VMEM((PIECES, rows, domain), F32),
            pltpu.VMEM((chips - 1, PIECES, rows, domain), F32),
            pltpu.VMEM((domain, domain), F32),
            dma((QUARTERS,)),
            dma((2,)),
            dma((3,)),
            dma((4,)),
            dma((3,)),
            dma((3,)),
            dma((PIECES,)),
            dma((PIECES,)),
            dma((chips - 1, PIECES)),
            dma((chips - 1, PIECES)),
            dma((PIECES,)),
            dma((PIECES,)),
        ],
        compiler_params=pltpu.CompilerParams(
            collective_id=0, has_side_effects=True, vmem_limit_bytes=VMEM_LIMIT
        ),
    )(attribute_order, table_rows, log_potential, measure_noise)
    updated, beliefs = pl.pallas_call(
        hand_on,
        out_shape=(table, table),
        in_specs=[hbm, hbm],
        out_specs=(hbm, hbm),
        scratch_shapes=[
            pltpu.VMEM((2, 2, domain // 2, domain), F32), dma((2, 2)), dma((2, 2)),
        ],
        compiler_params=pltpu.CompilerParams(vmem_limit_bytes=VMEM_LIMIT),
    )(updated, beliefs)
    return updated[None], beliefs[None]


def solution(mesh):
    in_specs = (P(None, "dp"), P(), P("clique", None, None), P("clique", None, None))
    out_specs = (P("clique", None, None), P("clique", None, None))
    return jax.shard_map(
        per_device, mesh=mesh, in_specs=in_specs, out_specs=out_specs, check_vma=False
    )
```
